32 devices in a mesh: seq: 4 (over y, x), expert: 8 (over z, core).
Axes of the slice: x: 2, y: 2, z: 4, core: 2. Of those that a mesh axis runs over, the one named last changes fastest.
Arguments:
- tokens: bfloat16 [8, 1024, 4096], P('expert', 'seq'), may hold values from -6 to 6
- norm_gain: float32 [4096], replicated, may hold values from 0.1 to 1.9
- conv_weight: float32 [4, 4096], replicated, may hold values from -3 to 3
- conv_bias: float32 [4096], replicated, may hold values from -3 to 3
- proj_weight: bfloat16 [4096, 288], replicated, may hold values from -0.09375 to 0.09375
- dt_weight: bfloat16 [256, 4096], replicated, may hold values from -0.375 to 0.375
- dt_bias: float32 [4096], replicated, may hold values from -4 to 0
- decay_rate: float32 [16, 4096], replicated, may hold values from 0.02 to 1
- skip_gain: float32 [4096], replicated, may hold values from 0.5 to 1.5
- ffn_gain: float32 [4096], replicated, may hold values from 0.1 to 1.9
- expert_ids: int32 [8, 1024, 2], P('expert', 'seq'), may hold values from 0 to 7, all different within a row; in each aligned block of 256 rows (0 to 255, 256 to 511, ..., all dimensions but the last counted through in order) at most 128 rows name the same one
- route_weights: float32 [8, 1024, 2], P('expert', 'seq'), may hold values from 0.2 to 1
- w_gate: bfloat16 [8, 4096, 512], P('expert'), may hold values from -0.09375 to 0.09375
- w_up: bfloat16 [8, 4096, 512], P('expert'), may hold values from -0.09375 to 0.09375
- w_down: bfloat16 [8, 512, 4096], P('expert'), may hold values from -0.25 to 0.25
Outputs:
- block_out: bfloat16 [8, 1024, 4096], P('expert', 'seq')
The draws below stay inside these ranges and needn't reach their ends.
Inputs may be any that keep to these rules, and one draw needn't show every extreme that they name: `expert_ids`: the two expert slices of a position differ. Among the 256 positions of one device, no expert slice is chosen more than 128 times, and in every draw some expert slice is chosen exactly 128 times by the positions of some device; every expert slice is chosen somewhere.
All inputs are finite; a program needn't handle non-finite values.
Results may differ from the reference program's by a relative error of at most 0.0085.
Values may be sent and summed in bfloat16 or wider, within the bound.
No kernel may reach another device: no remote copies, remote signals or barrier semaphores. Data moves between devices by JAX's collectives and lax.ppermute only.
A program may use at most 128 MiB of HBM per device.

```python
import math
import jax
import jax.numpy as jnp
import numpy as np
from jax import lax

D = 4096
FF = 512
STATE = 16
DT_RANK = 256
CONV = 4
TOK_DEV = 256
LEN = 1024
BATCH = 8
EXPERTS = 8
CAP = 128
N_SEQ = 4


def levels(key, dims, shards, least, high):
    def one(position, blocks):
        heights = jax.random.uniform(jax.random.fold_in(jax.random.fold_in(key, 6), position), (blocks,), jnp.float32, least / len(shards), high / len(shards))
        return jnp.repeat(jnp.exp(heights), dims[position] // blocks).reshape((-1,) + (1,) * (len(dims) - position - 1))

    level = one(*shards[0])
    for cut in shards[1:]:
        level = level * one(*cut)
    return level


def assign_block(stream_key, own, number, rows, count, top, reach, lean):
    ranking = jax.random.permutation(stream_key, count)
    heavy_load, common = load_shares(count, rows * top, reach, lean, True), load_shares(count, rows * top, reach, lean, False)
    places = jnp.arange(count)

    def named(tallies, turn):
        used = int((tallies > 0).sum())
        fixed = max(1, used // 4)
        shifted = fixed + (places - fixed + turn * (used - fixed)) % max(1, count - fixed)
        return jnp.zeros((count,), jnp.int32).at[ranking[jnp.where(places < fixed, places, shifted)]].set(jnp.asarray(tallies, jnp.int32))

    tallies = jnp.where(number % 4 == 0, named(heavy_load, number // 4), named(common, number - number // 4 - 1))
    mixed = jax.random.permutation(jax.random.fold_in(own, 3), count)
    donor, sink = mixed[0:count // 2 * 2:2], mixed[1:count // 2 * 2:2]
    margin = jnp.minimum(tallies[donor] - 1, reach - tallies[sink]) // 2
    margin = jnp.where((donor == ranking[0]) | (sink == ranking[0]) | (tallies[sink] == 0), 0, jnp.maximum(margin, 0))
    shifted = jax.random.randint(jax.random.fold_in(own, 4), (count // 2,), 0, 1 << 20) % (margin + 1)
    tallies = tallies.at[donor].add(-shifted).at[sink].add(shifted)
    members = jnp.searchsorted(jnp.cumsum(tallies), jnp.arange(rows * top), side="right").astype(jnp.int32)
    listing = members.reshape(top, rows).T
    listing = listing[jax.random.permutation(jax.random.fold_in(own, 1), rows)]
    turn = jax.random.randint(jax.random.fold_in(own, 2), (rows, 1), 0, top)
    return jnp.take_along_axis(listing, (jnp.arange(top)[None, :] + turn) % top, axis=1)


def load_shares(count, total, most, slope, full):
    weights = [(1 << 20) // math.isqrt(rank ** slope) + 1 for rank in range(1, count + 1)]
    largest = most if full else min(most, max(-(-total // count), total * weights[0] // sum(weights)))
    least = 1 if total - largest >= count - 1 else 0
    holding, rest = [largest] + [least] * (count - 1), total - largest - least * (count - 1)
    while rest > 0:
        free = [i for i in range(1, count) if holding[i] < largest] or [i for i in range(1, count) if holding[i] < most]
        mass, budget = sum([weights[i] for i in free]), rest
        for i in free:
            extra = min(most - holding[i], max(1, budget * weights[i] // mass), rest)
            holding[i] = holding[i] + extra
            rest = rest - extra
    return np.array(holding)


def normal_values(stream_key, dims, deviation, reach, shards=(), kind=jnp.bfloat16):
    values = deviation * jax.random.normal(stream_key, dims, jnp.float32)
    if shards:
        values = values * levels(stream_key, dims, shards, -0.22, 0.18)
    return jnp.clip(values, -reach, reach).astype(kind)


def setup_inputs(seed: int = 0) -> dict:
    key_list = jax.random.split(jax.random.key(seed), 16)
    tokens = normal_values(key_list[0], (BATCH, LEN, D), 1.0, 6.0, ((0, 8), (1, 4)))
    norm_gain = jnp.clip(1.0 + 0.18 * jax.random.normal(key_list[1], (D,), jnp.float32), 0.1, 1.9)
    conv_weight = normal_values(key_list[2], (CONV, D), CONV ** -0.5, 3.0, (), jnp.float32)
    conv_bias = normal_values(key_list[3], (D,), 0.5, 3.0, (), jnp.float32)
    proj_weight = normal_values(key_list[4], (D, DT_RANK + 2 * STATE), D ** -0.5, 0.09375)
    dt_weight = normal_values(key_list[5], (DT_RANK, D), DT_RANK ** -0.5, 0.375)
    dt_bias = jnp.clip(jax.random.uniform(key_list[6], (D,), jnp.float32, -4.0, 0.0), -4.0, 0.0)
    decay_rate = jnp.clip(jnp.exp(jax.random.uniform(key_list[7], (STATE, D), jnp.float32, math.log(0.02), math.log(1.0))), 0.02, 1.0)
    skip_gain = jnp.clip(jax.random.uniform(key_list[8], (D,), jnp.float32, 0.5, 1.5), 0.5, 1.5)
    ffn_gain = jnp.clip(1.0 + 0.18 * jax.random.normal(key_list[9], (D,), jnp.float32), 0.1, 1.9)
    expert_ids_keys = jax.random.split(jax.random.fold_in(key_list[10], 1), BATCH * LEN // TOK_DEV)
    expert_ids_turns = jax.random.permutation(jax.random.fold_in(key_list[10], 3), BATCH * LEN // TOK_DEV)
    expert_ids = jax.vmap(lambda own, number: assign_block(jax.random.fold_in(key_list[10], 2), own, number, TOK_DEV, EXPERTS, 2, CAP, 2))(expert_ids_keys, expert_ids_turns).reshape((BATCH, LEN, 2))
    route_weights = jnp.clip(0.2 + 0.8 * jax.random.uniform(key_list[11], (BATCH, LEN, 2), jnp.float32) ** levels(key_list[11], (BATCH, LEN, 2), ((0, 8), (1, 4)), -0.2, 0.2), 0.2, 1.0)
    w_gate = normal_values(key_list[12], (EXPERTS, D, FF), D ** -0.5, 0.09375, ((0, 8),))
    w_up = normal_values(key_list[13], (EXPERTS, D, FF), D ** -0.5, 0.09375, ((0, 8),))
    w_down = normal_values(key_list[14], (EXPERTS, FF, D), FF ** -0.5, 0.25, ((0, 8),))
    return {"tokens": tokens, "norm_gain": norm_gain, "conv_weight": conv_weight, "conv_bias": conv_bias, "proj_weight": proj_weight, "dt_weight": dt_weight, "dt_bias": dt_bias, "decay_rate": decay_rate, "skip_gain": skip_gain, "ffn_gain": ffn_gain, "expert_ids": expert_ids, "route_weights": route_weights, "w_gate": w_gate, "w_up": w_up, "w_down": w_down}


def rms_scale(values, gain):
    return values * lax.rsqrt(lax.optimization_barrier(jnp.mean(values * values, axis=-1, keepdims=True)) + 1e-05) * gain

def reference(tokens, norm_gain, conv_weight, conv_bias, proj_weight, dt_weight, dt_bias, decay_rate, skip_gain, ffn_gain, expert_ids, route_weights, w_gate, w_up, w_down):
    stream = tokens.astype(jnp.float32)
    normed = rms_scale(stream, norm_gain).astype(jnp.bfloat16)
    padded = jnp.pad(normed.astype(jnp.float32), ((0, 0), (CONV - 1, 0), (0, 0)))
    conv_sum = jnp.zeros((BATCH, LEN, D), jnp.float32)
    for offset in range(CONV):
        conv_sum = conv_sum + conv_weight[offset] * padded[:, offset:offset + LEN]
    conv_out = jax.nn.silu(conv_sum + conv_bias).astype(jnp.bfloat16)
    conv_rows = conv_out.reshape(BATCH * LEN, D)
    projected = jnp.dot(conv_rows, proj_weight, preferred_element_type=jnp.float32)
    low_rank = projected[:, :DT_RANK].astype(jnp.bfloat16)
    step_size = jax.nn.softplus(jnp.dot(low_rank, dt_weight, preferred_element_type=jnp.float32) + dt_bias)
    input_map = projected[:, DT_RANK:DT_RANK + STATE]
    output_map = projected[:, DT_RANK + STATE:]
    decay_neg = -decay_rate
    conv_float = conv_out.astype(jnp.float32)
    step_time = step_size.reshape(BATCH, LEN, D).transpose(1, 0, 2)
    conv_time = conv_float.transpose(1, 0, 2)
    input_time = input_map.reshape(BATCH, LEN, STATE).transpose(1, 0, 2)
    output_time = output_map.reshape(BATCH, LEN, STATE).transpose(1, 0, 2)

    def advance(ssm_state, pieces):
        step_now, input_now, in_now, out_now = pieces
        ssm_state = jnp.exp(step_now[:, None, :] * decay_neg) * ssm_state + (step_now * input_now)[:, None, :] * in_now[:, :, None]
        return (ssm_state, lax.optimization_barrier(jnp.sum(out_now[:, :, None] * ssm_state, axis=1)))
    _, collected = lax.scan(advance, jnp.zeros((BATCH, STATE, D), jnp.float32), (step_time, conv_time, input_time, output_time))
    scanned = collected.transpose(1, 0, 2)
    hidden_state = stream + (scanned + skip_gain * conv_float)
    ffn_in = rms_scale(hidden_state, ffn_gain).astype(jnp.bfloat16).reshape(BATCH * LEN, D)
    blocks = BATCH * N_SEQ
    pair_count = 2 * TOK_DEV
    chosen = expert_ids.reshape(blocks, pair_count).astype(jnp.int32)
    onehot = (chosen[:, :, None] == jnp.arange(EXPERTS, dtype=jnp.int32)[None, None, :]).astype(jnp.int32)
    before = jnp.cumsum(onehot, axis=1) - onehot
    slot_pos = lax.optimization_barrier(jnp.sum(before * onehot, axis=2)).astype(jnp.int32)
    block_index = jnp.broadcast_to(jnp.arange(blocks, dtype=jnp.int32)[:, None], (blocks, pair_count))
    assign = jnp.arange(blocks * pair_count, dtype=jnp.int32).reshape(blocks, pair_count)
    slot_table = jnp.full((EXPERTS, blocks, CAP), -1, jnp.int32).at[chosen, block_index, slot_pos].set(assign)
    weights_flat = route_weights.reshape(-1)

    def expert_pass(routed, pieces):
        rows_index, gate_mat, up_mat, down_mat = pieces
        rows_index = rows_index.reshape(-1)
        usable = rows_index >= 0
        clipped = jnp.where(usable, rows_index, 0).astype(jnp.int32)
        token_index = (clipped // 2).astype(jnp.int32)
        rows_in = jnp.where(usable[:, None], ffn_in[token_index], jnp.zeros((), ffn_in.dtype))
        gate_part = jnp.dot(rows_in, gate_mat, preferred_element_type=jnp.float32)
        up_part = jnp.dot(rows_in, up_mat, preferred_element_type=jnp.float32)
        inner_act = (jax.nn.silu(gate_part) * up_part).astype(jnp.bfloat16)
        result = jnp.dot(inner_act, down_mat, preferred_element_type=jnp.float32).astype(jnp.bfloat16).astype(jnp.float32)
        route_scale = jnp.where(usable, weights_flat[clipped], jnp.zeros((), weights_flat.dtype))
        return (routed.at[token_index].add(route_scale[:, None] * result), None)
    routed, _ = lax.scan(expert_pass, jnp.zeros((BATCH * LEN, D), jnp.float32), (slot_table, w_gate, w_up, w_down))
    block_out = (hidden_state.reshape(BATCH * LEN, D) + routed).astype(jnp.bfloat16)
    return block_out.reshape(BATCH, LEN, D)
```

```python
import functools
import math

import jax
import jax.numpy as jnp
from jax import lax
from jax.experimental import pallas as pl
from jax.experimental.pallas import tpu as pltpu
from jax.sharding import PartitionSpec as P

LANES = 128
GROUP = 8
LOG2E = math.log2(math.e)


def from_behind(array, axis, by):
    peers = lax.axis_size(axis)
    pairs = [(i, i + by) for i in range(peers) if 0 <= i + by < peers]
    return lax.ppermute(array, axis, pairs)


def silu(v):
    return v / (1.0 + jnp.exp(-v))


def softplus(v):
    return jnp.maximum(v, 0.0) + jnp.log1p(jnp.exp(-jnp.abs(v)))


def spread_columns(maps, target, first, count, rows):
    for n in range(count):
        target[n] = jnp.broadcast_to(maps[:, first + n : first + n + 1], (rows, LANES))


def front_kernel(
    tok_ref, halo_ref, norm_gain, conv_weight, conv_bias, low_weight, maps_weight,
    dt_weight, dt_bias, decay,
    conv_ref, step_ref, drive_ref, maps_ref, end_ref, total_ref,
    normed, low, block, in_rows,
):
    rows, width = tok_ref.shape
    halo = halo_ref.shape[0]
    states = decay.shape[0]
    taps = conv_weight.shape[0]
    tiles = width // LANES
    gain = norm_gain[...]

    def norm_rows(x):
        x = x.astype(jnp.float32)
        scale = lax.rsqrt(jnp.mean(x * x, axis=-1, keepdims=True) + 1e-05)
        return (x * scale * gain).astype(jnp.bfloat16).astype(jnp.float32)

    normed[pl.ds(0, halo), :] = norm_rows(halo_ref[...])

    def norm_step(i, _):
        at = pl.multiple_of(i * 16, 16)
        normed[pl.ds(halo + at, 16), :] = norm_rows(tok_ref[pl.ds(at, 16), :])
        return 0

    lax.fori_loop(0, rows // 16, norm_step, 0)

    chunk = 512

    def conv_step(i, _):
        at = pl.multiple_of(i * 16, 16)
        for c in range(width // chunk):
            cols = pl.ds(c * chunk, chunk)
            window = normed[pl.ds(pl.multiple_of(halo - 8 + at, 8), 24), cols]
            total = jnp.zeros((16, chunk), jnp.float32)
            for j in range(taps):
                back = taps - 1 - j
                moved = pltpu.roll(window, back, 0) if back else window
                total = total + conv_weight[pl.ds(j, 1), cols] * moved[8:24]
            conv_ref[pl.ds(at, 16), cols] = silu(total + conv_bias[:, cols]).astype(jnp.bfloat16)
        return 0

    lax.fori_loop(0, rows // 16, conv_step, 0)

    conv_all = conv_ref[...]
    low[...] = jnp.dot(
        conv_all, low_weight[...], preferred_element_type=jnp.float32
    ).astype(jnp.bfloat16)
    maps = jnp.dot(conv_all, maps_weight[...], preferred_element_type=jnp.float32)
    maps_ref[...] = maps
    spread_columns(maps, in_rows, 0, states, rows)

    def step_chunk(c, _):
        cols = pl.ds(pl.multiple_of(c * chunk, chunk), chunk)
        block[...] = softplus(
            jnp.dot(low[...], dt_weight[:, cols], preferred_element_type=jnp.float32)
            + dt_bias[:, cols]
        )

        def move(g, _):
            at = pl.multiple_of(g * 16, 16)
            step = block[pl.ds(at, 16), :]
            drive = step * conv_ref[pl.ds(at, 16), cols].astype(jnp.float32)
            for half in range(2):
                for j in range(chunk // LANES):
                    to = pl.ds((at + half * 8) * tiles + c * (chunk // LANES) + j, 8, stride=tiles)
                    part = (slice(half * 8, half * 8 + 8), slice(j * LANES, (j + 1) * LANES))
                    step_ref[to, :] = step[part]
                    drive_ref[to, :] = drive[part]
            return 0

        lax.fori_loop(0, rows // 16, move, 0)
        return 0

    lax.fori_loop(0, width // chunk, step_chunk, 0)

    def scan_tile(k, _):
        mine = pl.ds(pl.multiple_of(k * GROUP, GROUP), GROUP)
        rates = [decay[n, mine, :] for n in range(states)]

        def advance(i, carry):
            state, total = carry
            for p in range(4):
                t = i * 4 + p
                here = pl.ds(pl.multiple_of(t * tiles + k * GROUP, GROUP), GROUP)
                step, drive = step_ref[here, :], drive_ref[here, :]
                total = total + step
                state = tuple(
                    jnp.exp2(step * rates[n]) * state[n] + drive * in_rows[n, pl.ds(t, 1), :]
                    for n in range(states)
                )
            return state, total

        zero = jnp.zeros((GROUP, LANES), jnp.float32)
        state, total = lax.fori_loop(0, rows // 4, advance, ((zero,) * states, zero))
        for n in range(states):
            end_ref[n, mine, :] = state[n]
        total_ref[mine, :] = total
        return 0

    lax.fori_loop(0, tiles // GROUP, scan_tile, 0)


def back_kernel(
    tok_ref, conv_ref, step_ref, drive_ref, maps_ref, decay, skip_gain, ffn_gain, *rest,
    before,
):
    ends, totals = rest[:before], rest[before : 2 * before]
    hidden_ref, ffn_ref = rest[2 * before : 2 * before + 2]
    in_rows, out_rows, scanned = rest[2 * before + 2 :]
    rows, width = tok_ref.shape
    states = decay.shape[0]
    tiles = width // LANES
    maps = maps_ref[...]
    spread_columns(maps, in_rows, 0, states, rows)
    spread_columns(maps, out_rows, states, states, rows)

    def scan_tile(k, _):
        mine = pl.ds(pl.multiple_of(k * GROUP, GROUP), GROUP)
        rates = [decay[n, mine, :] for n in range(states)]
        start = []
        for n in range(states):
            entering = jnp.zeros((GROUP, LANES), jnp.float32)
            for back in reversed(range(before)):
                entering = (
                    jnp.exp2(totals[back][mine, :] * rates[n]) * entering
                    + ends[back][n, mine, :]
                )
            start.append(entering)

        def advance(i, state):
            for p in range(4):
                t = i * 4 + p
                here = pl.ds(pl.multiple_of(t * tiles + k * GROUP, GROUP), GROUP)
                step, drive = step_ref[here, :], drive_ref[here, :]
                state = tuple(
                    jnp.exp2(step * rates[n]) * state[n] + drive * in_rows[n, pl.ds(t, 1), :]
                    for n in range(states)
                )
                parts = [state[n] * out_rows[n, pl.ds(t, 1), :] for n in range(states)]
                while len(parts) > 1:
                    parts = [a + b for a, b in zip(parts[::2], parts[1::2])]
                scanned[here, :] = parts[0]
            return state

        lax.fori_loop(0, rows // 4, advance, tuple(start))
        return 0

    lax.fori_loop(0, tiles // GROUP, scan_tile, 0)

    def finish(i, _):
        at = pl.multiple_of(i * 16, 16)
        squares = jnp.zeros((16, LANES), jnp.float32)
        for j in range(tiles):
            cols = pl.ds(j * LANES, LANES)
            came = jnp.concatenate(
                [scanned[pl.ds((at + half * 8) * tiles + j, 8, stride=tiles), :] for half in range(2)],
                axis=0,
            )
            conv = conv_ref[pl.ds(at, 16), cols].astype(jnp.float32)
            hidden = tok_ref[pl.ds(at, 16), cols].astype(jnp.float32) + (
                came + skip_gain[:, cols] * conv
            )
            hidden_ref[pl.ds(at, 16), cols] = hidden
            squares = squares + hidden * hidden
        mean = jnp.sum(squares, axis=-1, keepdims=True) / width
        scale = lax.rsqrt(mean + 1e-05)
        ffn_ref[pl.ds(at, 16), :] = (
            hidden_ref[pl.ds(at, 16), :] * scale * ffn_gain[...]
        ).astype(jnp.bfloat16)
        return 0

    lax.fori_loop(0, rows // 16, finish, 0)


def mixer(
    tokens, norm_gain, conv_weight, conv_bias, proj_weight, dt_weight, dt_bias, decay_rate,
    skip_gain, ffn_gain,
):
    rows, width = tokens.shape
    states = decay_rate.shape[0]
    low_width = dt_weight.shape[0]
    tiles = width // LANES
    f32 = jnp.float32
    halo = from_behind(tokens[rows - 16 :], "seq", 1)
    decay = (decay_rate * (-LOG2E)).reshape(states, tiles, LANES)
    row = lambda v: v.reshape(1, width)
    conv, step, drive, maps, end, total = pl.pallas_call(
        front_kernel,
        out_shape=(
            jax.ShapeDtypeStruct((rows, width), jnp.bfloat16),
            jax.ShapeDtypeStruct((rows * tiles, LANES), f32),
            jax.ShapeDtypeStruct((rows * tiles, LANES), f32),
            jax.ShapeDtypeStruct((rows, 2 * states), f32),
            jax.ShapeDtypeStruct((states, tiles, LANES), f32),
            jax.ShapeDtypeStruct((tiles, LANES), f32),
        ),
        scratch_shapes=[
            pltpu.VMEM((rows + 16, width), f32),
            pltpu.VMEM((rows, low_width), jnp.bfloat16),
            pltpu.VMEM((rows, 512), f32),
            pltpu.VMEM((states, rows, LANES), f32),
        ],
        compiler_params=pltpu.CompilerParams(vmem_limit_bytes=56 * 2**20),
        cost_estimate=pl.CostEstimate(
            flops=2 * rows * width * (2 * low_width + 8 * states),
            bytes_accessed=20 * 2**20,
            transcendentals=rows * width * states,
        ),
        name="mixer_front",
    )(
        tokens, halo, row(norm_gain), conv_weight, row(conv_bias),
        proj_weight[:, :low_width], proj_weight[:, low_width:], dt_weight, row(dt_bias), decay,
    )
    before = lax.axis_size("seq") - 1
    ends = [from_behind(end, "seq", by + 1) for by in range(before)]
    totals = [from_behind(total, "seq", by + 1) for by in range(before)]
    hidden, ffn_in = pl.pallas_call(
        functools.partial(back_kernel, before=before),
        out_shape=(
            jax.ShapeDtypeStruct((rows, width), f32),
            jax.ShapeDtypeStruct((rows, width), jnp.bfloat16),
        ),
        scratch_shapes=[
            pltpu.VMEM((states, rows, LANES), f32),
            pltpu.VMEM((states, rows, LANES), f32),
            pltpu.VMEM((rows * tiles, LANES), f32),
        ],
        compiler_params=pltpu.CompilerParams(vmem_limit_bytes=56 * 2**20),
        cost_estimate=pl.CostEstimate(
            flops=2 * rows * width * 8 * states,
            bytes_accessed=20 * 2**20,
            transcendentals=rows * width * states,
        ),
        name="mixer_back",
    )(tokens, conv, step, drive, maps, decay, row(skip_gain), row(ffn_gain), *ends, *totals)
    return hidden, ffn_in


def routed_by_slots(ffn_in, chosen, route_scale, w_gate, w_up, w_down):
    tok_count, model_width = ffn_in.shape
    owners = lax.axis_size("expert")
    experts = owners * w_gate.shape[0]
    capacity = 4 * tok_count // owners
    chosen = chosen.reshape(-1)
    onehot = (chosen[:, None] == jnp.arange(experts, dtype=jnp.int32)[None, :]).astype(jnp.int32)
    before = jnp.cumsum(onehot, axis=0) - onehot
    slot_pos = jnp.sum(before * onehot, axis=1)
    dest_row = chosen * capacity + slot_pos
    outgoing = (
        jnp.zeros((experts * capacity, model_width), jnp.bfloat16)
        .at[dest_row]
        .set(jnp.repeat(ffn_in, 2, axis=0))
    )
    outgoing = outgoing.reshape(experts, capacity, model_width)
    received = lax.all_to_all(outgoing, "expert", split_axis=0, concat_axis=0, tiled=True)
    recv_shape = received.shape
    rows_in = received.reshape(-1, model_width)
    gate_part = jnp.dot(rows_in, w_gate[0], preferred_element_type=jnp.float32)
    up_part = jnp.dot(rows_in, w_up[0], preferred_element_type=jnp.float32)
    inner_act = (jax.nn.silu(gate_part) * up_part).astype(jnp.bfloat16)
    result = jnp.dot(inner_act, w_down[0], preferred_element_type=jnp.float32).astype(jnp.bfloat16)
    returned = lax.all_to_all(
        result.reshape(recv_shape), "expert", split_axis=0, concat_axis=0, tiled=True
    )
    gathered = returned.reshape(experts * capacity, model_width)[dest_row].astype(jnp.float32)
    weighted = (route_scale.reshape(-1)[:, None] * gathered).reshape(tok_count, 2, model_width)
    return weighted[:, 0] + weighted[:, 1]


def per_device(
    tokens, norm_gain, conv_weight, conv_bias, proj_weight, dt_weight, dt_bias, decay_rate,
    skip_gain, ffn_gain, expert_ids, route_weights, w_gate, w_up, w_down,
):
    hidden, ffn_in = mixer(
        tokens[0], norm_gain, conv_weight, conv_bias, proj_weight, dt_weight, dt_bias,
        decay_rate, skip_gain, ffn_gain,
    )
    routed = routed_by_slots(ffn_in, expert_ids[0], route_weights[0], w_gate, w_up, w_down)
    return (hidden + routed).astype(jnp.bfloat16)[None]


def solution(mesh):
    in_specs = (
        P("expert", "seq", None),
        P(), P(), P(), P(), P(), P(), P(), P(), P(),
        P("expert", "seq", None),
        P("expert", "seq", None),
        P("expert", None, None),
        P("expert", None, None),
        P("expert", None, None),
    )
    out_specs = P("expert", "seq", None)
    return jax.shard_map(
        per_device, mesh=mesh, in_specs=in_specs, out_specs=out_specs, check_vma=False
    )
```

```python
import functools
import math

import jax
import jax.numpy as jnp
from jax import lax
from jax.experimental import pallas as pl
from jax.experimental.pallas import tpu as pltpu
from jax.sharding import PartitionSpec as P

LANES = 128
GROUP = 8
LOG2E = math.log2(math.e)
VMEM_LIMIT = 56 * 2**20
COST = 0.5
DEEP = (1536, 1024, 1536)
BROAD = (1024, 1024, 1024, 1024)
PANEL = 1024
CORNERS_X = (0, 2)
STARTS = {
    "z1": ["front"], "x0": ["front"], "y0": ["front"], "w2": ["front"],
    "z2": ["ends"],
    "x1": ["e1", "e2", "e3"], "y1": ["e1", "e2", "e3"], "c0": ["e1", "e2", "e3"],
    "z3": ["back0"], "x2": ["back0"], "y2": ["back0"],
    "z4": ["back1"], "c1": ["back1"], "c2": ["back1"], "m0": ["t0"],
    "x3": ["n0"], "y3": ["n0"], "z5": ["n0"], "m1": ["n0"],
    "z6": ["near0"], "x4": ["near0"], "y4": ["near0"], "c3": ["near0"],
    "x5": ["far0"], "y5": ["far0"], "c4": ["far0"],
    "x6": ["near1"], "y6": ["near1"], "c5": ["near1"],
    "c6": ["far1"],
}
WAITS = {
    "front": ["z0", "w1"],
    "ends": ["x0", "y0", "z1", "w2"],
    "back0": ["z2", "x1", "y1"],
    "back1": ["z3", "x2", "y2", "c0"],
    "near0": ["x3", "y3", "z5", "m1"],
    "far0": ["x4", "y4", "c3", "z6"],
    "near1": ["x5", "y5", "c4"],
    "far1": ["x6", "y6", "c5"],
    "down0": ["c6"],
    "down1": ["s0"],
    "down2": ["s1"],
    "down3": ["s2", "r0"],
}


def from_behind(array, axis, by):
    peers = lax.axis_size(axis)
    pairs = [(i, i + by) for i in range(peers) if 0 <= i + by < peers]
    return lax.ppermute(array, axis, pairs)


def silu(v):
    return v / (1.0 + jnp.exp(-v))


def softplus(v):
    return jnp.maximum(v, 0.0) + jnp.log1p(jnp.exp(-jnp.abs(v)))


def spread_columns(maps, target, first, count, rows):
    for n in range(count):
        target[n] = jnp.broadcast_to(maps[:, first + n : first + n + 1], (rows, LANES))


def cost(micros):
    return pl.CostEstimate(flops=int(micros * 1.15e9), bytes_accessed=2**16, transcendentals=0)


def params():
    return pltpu.CompilerParams(vmem_limit_bytes=VMEM_LIMIT)


def front_kernel(
    tok_ref, halo_ref, norm_gain, conv_weight, conv_bias, proj_weight, dt_weight, dt_bias,
    conv_ref, step_ref, drive_ref, maps_ref,
    normed, low, block,
):
    rows, width = tok_ref.shape
    halo = halo_ref.shape[0]
    taps = conv_weight.shape[0]
    low_width = dt_weight.shape[0]
    tiles = width // LANES
    gain = norm_gain[...]

    def norm_rows(x):
        x = x.astype(jnp.float32)
        scale = lax.rsqrt(jnp.mean(x * x, axis=-1, keepdims=True) + 1e-05)
        return (x * scale * gain).astype(jnp.bfloat16).astype(jnp.float32)

    normed[pl.ds(0, halo), :] = norm_rows(halo_ref[...])

    def norm_step(i, _):
        at = pl.multiple_of(i * 16, 16)
        normed[pl.ds(halo + at, 16), :] = norm_rows(tok_ref[pl.ds(at, 16), :])
        return 0

    lax.fori_loop(0, rows // 16, norm_step, 0)

    chunk = 512

    def conv_step(i, _):
        at = pl.multiple_of(i * 16, 16)
        for c in range(width // chunk):
            cols = pl.ds(c * chunk, chunk)
            window = normed[pl.ds(pl.multiple_of(halo - 8 + at, 8), 24), cols]
            total = jnp.zeros((16, chunk), jnp.float32)
            for j in range(taps):
                back = taps - 1 - j
                moved = pltpu.roll(window, back, 0) if back else window
                total = total + conv_weight[pl.ds(j, 1), cols] * moved[8:24]
            conv_ref[pl.ds(at, 16), cols] = silu(total + conv_bias[:, cols]).astype(jnp.bfloat16)
        return 0

    lax.fori_loop(0, rows // 16, conv_step, 0)

    conv_all = conv_ref[...]
    low[...] = jnp.dot(
        conv_all, proj_weight[:, :low_width], preferred_element_type=jnp.float32
    ).astype(jnp.bfloat16)
    maps_ref[...] = jnp.dot(
        conv_all, proj_weight[:, low_width:], preferred_element_type=jnp.float32
    )

    def step_chunk(c, _):
        cols = pl.ds(pl.multiple_of(c * chunk, chunk), chunk)
        block[...] = softplus(
            jnp.dot(low[...], dt_weight[:, cols], preferred_element_type=jnp.float32)
            + dt_bias[:, cols]
        )

        def move(g, _):
            at = pl.multiple_of(g * 16, 16)
            step = block[pl.ds(at, 16), :]
            drive = step * conv_ref[pl.ds(at, 16), cols].astype(jnp.float32)
            for half in range(2):
                for j in range(chunk // LANES):
                    to = pl.ds((at + half * 8) * tiles + c * (chunk // LANES) + j, 8, stride=tiles)
                    part = (slice(half * 8, half * 8 + 8), slice(j * LANES, (j + 1) * LANES))
                    step_ref[to, :] = step[part]
                    drive_ref[to, :] = drive[part]
            return 0

        lax.fori_loop(0, rows // 16, move, 0)
        return 0

    lax.fori_loop(0, width // chunk, step_chunk, 0)


def advance_state(state, step, drive, rates, in_rows, t):
    return tuple(
        jnp.exp2(step * rates[n]) * state[n] + drive * in_rows[n, pl.ds(t, 1), :]
        for n in range(len(rates))
    )


def ends_kernel(step_ref, drive_ref, maps_ref, decay, end_ref, in_rows):
    rows = step_ref.shape[0]
    states = decay.shape[0]

    @pl.when(pl.program_id(0) == 0)
    def _():
        spread_columns(maps_ref[...], in_rows, 0, states, rows)

    rates = [decay[n] for n in range(states)]

    def advance(i, carry):
        state, total = carry
        for p in range(4):
            t = i * 4 + p
            step = step_ref[t]
            total = total + step
            state = advance_state(state, step, drive_ref[t], rates, in_rows, t)
        return state, total

    zero = jnp.zeros((GROUP, LANES), jnp.float32)
    state, total = lax.fori_loop(0, rows // 4, advance, ((zero,) * states, zero))
    for n in range(states):
        end_ref[n] = state[n]
    end_ref[states] = total


def back_kernel(
    tok_ref, conv_ref, step_ref, drive_ref, maps_ref, decay, skip_gain, ffn_gain, *rest,
    before, final,
):
    count = max(before, 1)
    entry, rest = rest[:count], rest[count:]
    if final:
        hidden_ref, ffn_ref, kept, in_rows, out_rows, scanned = rest
    else:
        hidden_ref, ffn_ref, state_ref, kept, in_rows, out_rows, scanned = rest
    rows, width = tok_ref.shape
    states = decay.shape[0]
    tiles = width // LANES
    maps = maps_ref[...]
    spread_columns(maps, in_rows, 0, states, rows)
    spread_columns(maps, out_rows, states, states, rows)

    @pl.when(pl.program_id(0) == 0)
    def _():
        if not before:
            kept[...] = entry[0][...]
            return

        def enter(n, _):
            entering = entry[before - 1][n]
            for back in reversed(range(before - 1)):
                entering = jnp.exp2(entry[back][states] * decay[n]) * entering + entry[back][n]
            kept[n] = entering
            return 0

        lax.fori_loop(0, states, enter, 0)

    def scan_tile(k, _):
        mine = pl.ds(pl.multiple_of(k * GROUP, GROUP), GROUP)
        rates = [decay[n, mine, :] for n in range(states)]

        def advance(i, state):
            for p in range(4):
                t = i * 4 + p
                state = advance_state(
                    state, step_ref[t, mine, :], drive_ref[t, mine, :], rates, in_rows, t
                )
                parts = [state[n] * out_rows[n, pl.ds(t, 1), :] for n in range(states)]
                while len(parts) > 1:
                    parts = [a + b for a, b in zip(parts[::2], parts[1::2])]
                scanned[pl.ds(pl.multiple_of(t * tiles + k * GROUP, GROUP), GROUP), :] = parts[0]
            return state

        state = lax.fori_loop(0, rows // 4, advance, tuple(kept[n, mine, :] for n in range(states)))
        for n in range(states):
            kept[n, mine, :] = state[n]
        return 0

    lax.fori_loop(0, tiles // GROUP, scan_tile, 0)
    if not final:
        state_ref[...] = kept[...]

    def finish(i, _):
        at = pl.multiple_of(i * 16, 16)
        squares = jnp.zeros((16, LANES), jnp.float32)
        for j in range(tiles):
            cols = pl.ds(j * LANES, LANES)
            came = jnp.concatenate(
                [scanned[pl.ds((at + half * 8) * tiles + j, 8, stride=tiles), :] for half in range(2)],
                axis=0,
            )
            conv = conv_ref[pl.ds(at, 16), cols].astype(jnp.float32)
            hidden = tok_ref[pl.ds(at, 16), cols].astype(jnp.float32) + (
                came + skip_gain[:, cols] * conv
            )
            hidden_ref[pl.ds(at, 16), cols] = hidden
            squares = squares + hidden * hidden
        mean = jnp.sum(squares, axis=-1, keepdims=True) / width
        scale = lax.rsqrt(mean + 1e-05)
        ffn_ref[pl.ds(at, 16), :] = (
            hidden_ref[pl.ds(at, 16), :] * scale * ffn_gain[...]
        ).astype(jnp.bfloat16)
        return 0

    lax.fori_loop(0, rows // 16, finish, 0)


def mixer(
    tokens, norm_gain, conv_weight, conv_bias, proj_weight, dt_weight, dt_bias, decay_rate,
    skip_gain, ffn_gain, parts, hold, note,
):
    rows, width = tokens.shape
    states = decay_rate.shape[0]
    low_width = dt_weight.shape[0]
    tiles = width // LANES
    f32, bf16 = jnp.float32, jnp.bfloat16
    shape = jax.ShapeDtypeStruct
    halo = from_behind(tokens[rows - 16 :], "seq", 1)
    decay = (decay_rate * (-LOG2E)).reshape(states, tiles, LANES)
    row = lambda v: v.reshape(1, width)
    conv, step, drive, maps = pl.pallas_call(
        front_kernel,
        out_shape=(
            shape((rows, width), bf16),
            shape((rows * tiles, LANES), f32),
            shape((rows * tiles, LANES), f32),
            shape((rows, 2 * states), f32),
        ),
        scratch_shapes=[
            pltpu.VMEM((rows + 16, width), f32),
            pltpu.VMEM((rows, low_width), bf16),
            pltpu.VMEM((rows, 512), f32),
        ],
        compiler_params=params(),
        cost_estimate=cost(COST),
        name="mixer_front",
    )(
        tokens, halo, row(norm_gain), conv_weight, row(conv_bias),
        proj_weight, dt_weight, row(dt_bias),
    )
    conv, step, drive, maps = hold("front", conv, step, drive, maps)
    step = step.reshape(rows, tiles, LANES)
    drive = drive.reshape(rows, tiles, LANES)
    slab = pl.BlockSpec((rows, GROUP, LANES), lambda k: (0, k, 0))
    per_state = pl.BlockSpec((states, GROUP, LANES), lambda k: (0, k, 0))
    ended = pl.BlockSpec((states + 1, GROUP, LANES), lambda k: (0, k, 0))
    end = pl.pallas_call(
        ends_kernel,
        grid=(tiles // GROUP,),
        out_shape=shape((states + 1, tiles, LANES), f32),
        in_specs=[slab, slab, pl.BlockSpec((rows, 2 * states), lambda k: (0, 0)), per_state],
        out_specs=ended,
        scratch_shapes=[pltpu.VMEM((states, rows, LANES), f32)],
        compiler_params=params(),
        cost_estimate=cost(COST),
        name="mixer_ends",
    )(step, drive, maps, decay)
    end, = hold("ends", end)
    before = lax.axis_size("seq") - 1
    ends = [note(f"e{by + 1}", from_behind(end, "seq", by + 1)) for by in range(before)]

    count = rows // parts
    piece = min(64, count)
    steps = count // piece
    outs = []
    state = None
    for part in range(parts):
        first = part * steps
        wide = pl.BlockSpec((piece, width), lambda i, first=first: (first + i, 0))
        deep = pl.BlockSpec((piece, tiles, LANES), lambda i, first=first: (first + i, 0, 0))
        narrow = pl.BlockSpec((piece, 2 * states), lambda i, first=first: (first + i, 0))
        whole = lambda v: pl.BlockSpec(v.shape, lambda i, r=v.ndim: (0,) * r)
        out = pl.BlockSpec((piece, width), lambda i: (i, 0))
        entry = ends if part == 0 else [state]
        final = part == parts - 1
        fixed = [decay, row(skip_gain), row(ffn_gain), *entry]
        got = pl.pallas_call(
            functools.partial(back_kernel, before=before if part == 0 else 0, final=final),
            grid=(steps,),
            out_shape=(shape((count, width), f32), shape((count, width), bf16))
            + (() if final else (shape(decay.shape, f32),)),
            in_specs=[wide, wide, deep, deep, narrow] + [whole(v) for v in fixed],
            out_specs=(out, out) + (() if final else (whole(decay),)),
            scratch_shapes=[
                pltpu.VMEM((states, tiles, LANES), f32),
                pltpu.VMEM((states, piece, LANES), f32),
                pltpu.VMEM((states, piece, LANES), f32),
                pltpu.VMEM((piece * tiles, LANES), f32),
            ],
            compiler_params=params(),
            cost_estimate=cost(COST),
            name="mixer_back",
        )(tokens, conv, step, drive, maps, *fixed)
        got = hold(f"back{part}", *got)
        outs.append(got[:2])
        state = got[2] if not final else None
    return [o[0] for o in outs], [o[1] for o in outs]


def swap(array, axis, mask):
    peers = lax.axis_size(axis)
    return lax.ppermute(array, axis, [(i, i ^ mask) for i in range(peers)])


def after(array, *others):
    return lax.optimization_barrier((array, *others))[0]


class Transfers:
    def __init__(self, w_gate, w_up, w_down):
        share = w_gate.shape[1] // lax.axis_size("seq")
        at = lax.axis_index("seq") * share
        both = jnp.concatenate(
            [lax.dynamic_slice_in_dim(w, at, share, axis=1) for w in (w_gate, w_up)], axis=1
        )
        down = lax.dynamic_slice_in_dim(w_down, at, share, axis=0)
        self.chunks = []
        for whole, sizes, axis in ((both, DEEP, 0), (down, BROAD, 1)):
            at = 0
            for size in sizes:
                self.chunks.append(lax.slice_in_dim(whole, at, at + size, axis=axis))
                at += size
        self.made = {}

    def put(self, name, array, axis, mask):
        self.made[name] = swap(self.ready(name, array), axis, mask)
        return self.made[name]

    def ready(self, name, array):
        return after(array, *[self.get(other) for other in STARTS.get(name, ())])

    def note(self, name, array):
        self.made[name] = array
        return array

    def weigh(self, chosen, route_scale):
        experts = jnp.arange(lax.axis_size("expert"), dtype=jnp.int32)[:, None, None]
        self.dense = jnp.sum(jnp.where(chosen[None] == experts, route_scale[None], 0.0), axis=2)

    def get(self, name):
        if name not in self.made:
            kind, c = name[0], int(name[1:])
            if name == "w1":
                send, axis, mask = self.dense, "expert", 1
            elif name == "w2":
                self.pair = jnp.concatenate([self.dense, self.get("w1")], axis=1)
                send, axis, mask = self.pair, "expert", 2
            elif kind == "z":
                send, axis, mask = self.chunks[c], "expert", 4
            elif kind == "x":
                send, axis, mask = self.get(f"z{c}"), "seq", 1
            elif kind == "y":
                send, axis, mask = self.get(f"z{c}"), "seq", 2
            elif c in CORNERS_X:
                send, axis, mask = self.get(f"y{c}"), "seq", 1
            else:
                send, axis, mask = self.get(f"x{c}"), "seq", 2
            self.put(name, send, axis, mask)
        return self.made[name]

    def pieces(self, c):
        return [self.get(f"{kind}{c}") for kind in "zxyc"]

    def hold(self, kernel, *arrays):
        self.made[kernel] = arrays[-1]
        others = [self.get(name) for name in WAITS.get(kernel, ())]
        return lax.optimization_barrier((*arrays, *others))[: len(arrays)]


def near_act_kernel(*refs, blocks):
    xs, (gate, up, scale, act_ref, rows_in) = refs[:blocks], refs[blocks:]
    count = xs[0].shape[0]

    @pl.when(pl.program_id(0) == 0)
    def _():
        for b in range(blocks):
            rows_in[b * count : (b + 1) * count, :] = xs[b][...]

    g = jnp.dot(rows_in[...], gate[...], preferred_element_type=jnp.float32)
    u = jnp.dot(rows_in[...], up[...], preferred_element_type=jnp.float32)
    act_ref[...] = (silu(g) * u * scale[:, 0:1]).astype(jnp.bfloat16)


def near_act(xs, w_gate, w_up, scale):
    rows = sum(x.shape[0] for x in xs)
    width, hidden = w_gate.shape
    tile = 256
    whole = lambda v: pl.BlockSpec(v.shape, lambda i: (0, 0))
    cols = pl.BlockSpec((width, tile), lambda i: (0, i))
    return pl.pallas_call(
        functools.partial(near_act_kernel, blocks=len(xs)),
        grid=(hidden // tile,),
        out_shape=jax.ShapeDtypeStruct((rows, hidden), jnp.bfloat16),
        in_specs=[whole(x) for x in xs] + [cols, cols, whole(scale)],
        out_specs=pl.BlockSpec((rows, tile), lambda i: (0, i)),
        scratch_shapes=[pltpu.VMEM((rows, width), jnp.bfloat16)],
        compiler_params=params(),
        cost_estimate=cost(COST),
        name="near_act",
    )(*xs, w_gate, w_up, scale)


def far_act_kernel(*refs, blocks, deep):
    xs, refs = refs[:blocks], refs[blocks:]
    weights, (scale, act_ref, rows_in) = refs[: 4 * deep], refs[4 * deep :]
    count = xs[0].shape[0]
    for b in range(blocks):
        rows_in[b * count : (b + 1) * count, :] = xs[b][...]
    share = weights[0].shape[1] // 2
    for origin in range(4):
        total, at = None, 0
        for c in range(deep):
            weight = weights[4 * c + origin]
            term = jnp.dot(
                rows_in[:, at : at + weight.shape[0]], weight[...],
                preferred_element_type=jnp.float32,
            )
            total = term if total is None else total + term
            at += weight.shape[0]
        act_ref[:, origin * share : (origin + 1) * share] = (
            silu(total[:, :share]) * total[:, share:] * scale[:, 1:2]
        ).astype(jnp.bfloat16)


def far_act(xs, chunks, scale):
    rows = sum(x.shape[0] for x in xs)
    width = xs[0].shape[1]
    share = chunks[0][0].shape[1] // 2
    pieces = [piece for chunk in chunks for piece in chunk]
    return pl.pallas_call(
        functools.partial(far_act_kernel, blocks=len(xs), deep=len(chunks)),
        out_shape=jax.ShapeDtypeStruct((rows, 4 * share), jnp.bfloat16),
        scratch_shapes=[pltpu.VMEM((rows, width), jnp.bfloat16)],
        compiler_params=params(),
        cost_estimate=cost(COST),
        name="far_act",
    )(*xs, *pieces, scale)


def down_kernel(*refs, halves):
    nears, fars, refs = refs[:halves], refs[halves : 2 * halves], refs[2 * halves :]
    near_weight, pieces, (keep_ref, send_ref) = refs[0], refs[1:5], refs[5:]
    far_weight = jnp.concatenate([p[...] for p in pieces], axis=0)
    for h in range(halves):
        total = jnp.dot(nears[h][...], near_weight[...], preferred_element_type=jnp.float32)
        total = total + jnp.dot(fars[h][...], far_weight, preferred_element_type=jnp.float32)
        count = total.shape[0] // 4
        own, mate, ahead, ahead_mate = [total[b * count : (b + 1) * count] for b in range(4)]
        rows = count * halves
        keep_ref[h * count : (h + 1) * count, :] = own
        keep_ref[rows + h * count : rows + (h + 1) * count, :] = ahead
        send_ref[h * count : (h + 1) * count, :] = mate.astype(jnp.bfloat16)
        send_ref[rows + h * count : rows + (h + 1) * count, :] = ahead_mate.astype(jnp.bfloat16)


def down(nears, fars, w_down, pieces, c, panel):
    cols, share = PANEL, pieces[0].shape[0]
    hidden = w_down.shape[0]
    rows = 2 * sum(a.shape[0] // 4 for a in nears)
    whole = lambda v: pl.BlockSpec(v.shape, lambda i: (0, 0))
    fixed = [*nears, *fars]
    return pl.pallas_call(
        functools.partial(down_kernel, halves=len(nears)),
        grid=(1,),
        out_shape=(
            jax.ShapeDtypeStruct((rows, cols), jnp.float32),
            jax.ShapeDtypeStruct((rows, cols), jnp.bfloat16),
        ),
        in_specs=[whole(v) for v in fixed]
        + [pl.BlockSpec((hidden, cols), lambda i: (0, c))]
        + [pl.BlockSpec((share, cols), lambda i: (0, panel)) for _ in pieces],
        out_specs=(
            pl.BlockSpec((rows, cols), lambda i: (0, 0)),
            pl.BlockSpec((rows, cols), lambda i: (0, 0)),
        ),
        compiler_params=params(),
        cost_estimate=cost(COST),
        name="down",
    )(*fixed, w_down, *pieces)


def routed_by_weights(hidden, ffn_in, w_gate, w_up, w_down, moves):
    me = lax.axis_index("expert")
    far = moves.get("w2")
    group = jnp.concatenate([moves.pair, far], axis=1)
    scale = jnp.stack([group[me], group[me ^ 4]], axis=1)
    rows = hidden[0].shape[0] * len(hidden)
    halves = len(ffn_in)
    count = rows // halves
    nears, fars = [], []
    order = None
    ahead = [moves.put(f"t{h}", ffn_in[h], "expert", 2) for h in range(halves)]
    for h in range(halves):
        mate = moves.put(f"m{h}", ffn_in[h], "expert", 1)
        ahead_mate = moves.put(f"n{h}", ahead[h], "expert", 1)
        xs = [ffn_in[h], mate, ahead[h], ahead_mate]
        part = scale.reshape(4, halves, count, 2)[:, h].reshape(4 * count, 2)
        part = part if order is None else after(part, order)
        near, = moves.hold(f"near{h}", near_act(xs, w_gate, w_up, part))
        nears.append(near)
        deep_chunks = [moves.pieces(c) for c in range(len(DEEP))]
        order, = moves.hold(f"far{h}", far_act(xs, deep_chunks, after(part, near)))
        fars.append(order)
    columns = []
    whole_hidden = jnp.concatenate(hidden, axis=0)
    for c, wide in enumerate(BROAD):
        pieces = moves.pieces(len(DEEP) + c)
        for panel in range(wide // PANEL):
            d = len(columns)
            cols = slice(d * PANEL, (d + 1) * PANEL)
            held = [after(pieces[0], order), *pieces[1:]]
            keep, send = moves.hold(f"down{d}", *down(nears, fars, w_down, held, d, panel))
            order = send
            came = moves.put(f"s{d}", send, "expert", 1).astype(jnp.float32)
            back = (keep[rows:] + came[rows:]).astype(jnp.bfloat16)
            back = moves.put(f"r{d}", back, "expert", 2).astype(jnp.float32)
            columns.append(whole_hidden[:, cols] + ((keep[:rows] + came[:rows]) + back))
    return jnp.concatenate(columns, axis=1)


def routed_by_slots(ffn_in, chosen, route_scale, w_gate, w_up, w_down):
    tok_count, model_width = ffn_in.shape
    owners = lax.axis_size("expert")
    experts = owners * w_gate.shape[0]
    capacity = 4 * tok_count // owners
    chosen = chosen.reshape(-1)
    onehot = (chosen[:, None] == jnp.arange(experts, dtype=jnp.int32)[None, :]).astype(jnp.int32)
    before = jnp.cumsum(onehot, axis=0) - onehot
    slot_pos = jnp.sum(before * onehot, axis=1)
    dest_row = chosen * capacity + slot_pos
    outgoing = (
        jnp.zeros((experts * capacity, model_width), jnp.bfloat16)
        .at[dest_row]
        .set(jnp.repeat(ffn_in, 2, axis=0))
    )
    outgoing = outgoing.reshape(experts, capacity, model_width)
    received = lax.all_to_all(outgoing, "expert", split_axis=0, concat_axis=0, tiled=True)
    recv_shape = received.shape
    rows_in = received.reshape(-1, model_width)
    gate_part = jnp.dot(rows_in, w_gate[0], preferred_element_type=jnp.float32)
    up_part = jnp.dot(rows_in, w_up[0], preferred_element_type=jnp.float32)
    inner_act = (jax.nn.silu(gate_part) * up_part).astype(jnp.bfloat16)
    result = jnp.dot(inner_act, w_down[0], preferred_element_type=jnp.float32).astype(jnp.bfloat16)
    returned = lax.all_to_all(
        result.reshape(recv_shape), "expert", split_axis=0, concat_axis=0, tiled=True
    )
    gathered = returned.reshape(experts * capacity, model_width)[dest_row].astype(jnp.float32)
    weighted = (route_scale.reshape(-1)[:, None] * gathered).reshape(tok_count, 2, model_width)
    return weighted[:, 0] + weighted[:, 1]


def per_device(
    tokens, norm_gain, conv_weight, conv_bias, proj_weight, dt_weight, dt_bias, decay_rate,
    skip_gain, ffn_gain, expert_ids, route_weights, w_gate, w_up, w_down,
):
    by_weights = lax.axis_size("expert") == 8 and lax.axis_size("seq") == 4
    hold = lambda kernel, *arrays: arrays
    note = lambda name, array: array
    if by_weights:
        moves = Transfers(w_gate[0], w_up[0], w_down[0])
        moves.weigh(expert_ids[0], route_weights[0])
        hold, note = moves.hold, moves.note
    hidden, ffn_in = mixer(
        tokens[0], norm_gain, conv_weight, conv_bias, proj_weight, dt_weight, dt_bias,
        decay_rate, skip_gain, ffn_gain, 2 if by_weights else 1, hold, note,
    )
    if by_weights:
        out = routed_by_weights(
            hidden, ffn_in, w_gate[0], w_up[0], w_down[0], moves
        )
    else:
        out = hidden[0] + routed_by_slots(
            ffn_in[0], expert_ids[0], route_weights[0], w_gate, w_up, w_down
        )
    return out.astype(jnp.bfloat16)[None]


def solution(mesh):
    in_specs = (
        P("expert", "seq", None),
        P(), P(), P(), P(), P(), P(), P(), P(), P(),
        P("expert", "seq", None),
        P("expert", "seq", None),
        P("expert", None, None),
        P("expert", None, None),
        P("expert", None, None),
    )
    out_specs = P("expert", "seq", None)
    return jax.shard_map(
        per_device, mesh=mesh, in_specs=in_specs, out_specs=out_specs, check_vma=False
    )
```

```python
import functools
import math

import jax
import jax.numpy as jnp
from jax import lax
from jax.experimental import pallas as pl
from jax.experimental.pallas import tpu as pltpu
from jax.sharding import PartitionSpec as P

LANES = 128
GROUP = 8
LOG2E = math.log2(math.e)
VMEM_LIMIT = 56 * 2**20
COST = 0.3
MERGE = False
TOGETHER = False
IN_TURN = False
DEEP = (1024, 1024, 768, 1280)
BROAD = (2048, 1024, 1024)
PANEL = 1024
CORNERS_X = (0, 2)
DIRECT = ()
STARTS = {'z0': ['w1', 'w2', 'w3'], 'z1': ['front'], 'x0': ['front'], 'y0': ['front'], 'c0': ['ends'], 'x1': ['e1', 'e2', 'e3'], 'y1': ['e1', 'e2', 'e3'], 'z2': ['e1', 'e2', 'e3', 'z1'], 'z3': ['back0'], 'x2': ['back0'], 'y2': ['back0'], 'c1': ['back0'], 'c2': ['back1'], 'm0': ['back1'], 'z4': ['z3', 'c1'], 'x3': ['z3', 'c2'], 'y3': ['z3'], 'c3': ['near0'], 'm1': ['near0'], 'z5': ['near0', 'z4'], 'x4': ['near0'], 'y4': ['near0'], 'c4': ['far0'], 'z6': ['far0'], 'x5': ['far0'], 'y5': ['y1'], 'c5': ['act1'], 'x6': ['act1'], 'y6': ['act1'], 'c6': ['down0'], 't1': ['front'], 'r2': ['s0']}
WAITS = {'front': ['z0'], 'ends': ['x0', 'y0'], 'back0': ['c0', 'y1', 'z2'], 'back1': ['x2', 'y2', 'c1'], 'near0': ['z4', 'x3', 'y3'], 'far0': ['z5', 'y4'], 'act1': ['x4', 'z6', 'x5', 'x6'], 'down0': ['c5'], 'down1': ['c6'], 'down2': ['y5', 'y6', 'r0'], 'down3': ['c4', 'r1']}


def from_behind(array, axis, by):
    peers = lax.axis_size(axis)
    pairs = [(i, i + by) for i in range(peers) if 0 <= i + by < peers]
    return lax.ppermute(array, axis, pairs)


def silu(v):
    return v / (1.0 + jnp.exp(-v))


def softplus(v):
    return jnp.maximum(v, 0.0) + jnp.log(1.0 + jnp.exp(-jnp.abs(v)))


def spread_columns(maps, target, first, count, rows):
    for n in range(count):
        target[n] = jnp.broadcast_to(maps[:, first + n : first + n + 1], (rows, LANES))


def cost(micros):
    return pl.CostEstimate(flops=int(micros * 1.15e9), bytes_accessed=2**16, transcendentals=0)


def params():
    return pltpu.CompilerParams(vmem_limit_bytes=VMEM_LIMIT)


def front_kernel(
    tok_ref, halo_ref, norm_gain, conv_weight, conv_bias, proj_weight, dt_weight, dt_bias,
    conv_ref, step_ref, drive_ref, maps_ref,
    normed, low, block,
):
    rows, width = tok_ref.shape
    halo = halo_ref.shape[0]
    taps = conv_weight.shape[0]
    low_width = dt_weight.shape[0]
    chunk = block.shape[1]
    part = pl.program_id(0)

    @pl.when(part == 0)
    def _():
        gain = norm_gain[...]

        def norm_rows(x):
            x = x.astype(jnp.float32)
            scale = lax.rsqrt(jnp.mean(x * x, axis=-1, keepdims=True) + 1e-05)
            return (x * scale * gain).astype(jnp.bfloat16).astype(jnp.float32)

        normed[pl.ds(0, halo), :] = norm_rows(halo_ref[...])

        def norm_step(i, _):
            at = pl.multiple_of(i * 16, 16)
            normed[pl.ds(halo + at, 16), :] = norm_rows(tok_ref[pl.ds(at, 16), :])
            return 0

        lax.fori_loop(0, rows // 16, norm_step, 0)

        def conv_step(i, _):
            at = pl.multiple_of(i * 16, 16)
            for c in range(width // chunk):
                cols = pl.ds(c * chunk, chunk)
                window = normed[pl.ds(pl.multiple_of(halo - 8 + at, 8), 24), cols]
                total = jnp.zeros((16, chunk), jnp.float32)
                for j in range(taps):
                    back = taps - 1 - j
                    moved = pltpu.roll(window, back, 0) if back else window
                    total = total + conv_weight[pl.ds(j, 1), cols] * moved[8:24]
                conv_ref[pl.ds(at, 16), cols] = silu(total + conv_bias[:, cols]).astype(
                    jnp.bfloat16
                )
            return 0

        lax.fori_loop(0, rows // 16, conv_step, 0)

        conv_all = conv_ref[...]
        project = lambda weight: lax.dot_general(
            conv_all, weight, (((1,), (1,)), ((), ())), preferred_element_type=jnp.float32
        )
        low[...] = project(proj_weight[:low_width, :]).astype(jnp.bfloat16)
        maps_ref[...] = project(proj_weight[low_width:, :])

    own = dt_weight.shape[1]
    for c in range(own // chunk):
        cols = slice(c * chunk, (c + 1) * chunk)
        block[...] = softplus(
            jnp.dot(low[...], dt_weight[:, cols], preferred_element_type=jnp.float32)
            + dt_bias[:, cols]
        )
        first = pl.multiple_of(part * own + c * chunk, chunk)

        def move(g, _):
            at = pl.multiple_of(g * 16, 16)
            step = block[pl.ds(at, 16), :]
            drive = step * conv_ref[pl.ds(at, 16), pl.ds(first, chunk)].astype(jnp.float32)
            for half in range(2):
                for j in range(chunk // LANES):
                    lane = c * (chunk // LANES) + j
                    to = pl.ds((at + half * 8) * GROUP + lane, 8, stride=GROUP)
                    part = (slice(half * 8, half * 8 + 8), slice(j * LANES, (j + 1) * LANES))
                    step_ref[to, :] = step[part]
                    drive_ref[to, :] = drive[part]
            return 0

        lax.fori_loop(0, rows // 16, move, 0)


def advance_state(state, step, drive, rates, in_rows, t):
    return tuple(
        jnp.exp2(step * rates[n]) * state[n] + drive * in_rows[n, pl.ds(t, 1), :]
        for n in range(len(rates))
    )


def ends_kernel(step_ref, drive_ref, maps_ref, decay, end_ref, in_rows):
    rows = step_ref.shape[0]
    states = decay.shape[0]

    @pl.when(pl.program_id(0) == 0)
    def _():
        spread_columns(maps_ref[...], in_rows, 0, states, rows)

    rates = [decay[n] for n in range(states)]

    def advance(i, carry):
        state, total = carry
        for p in range(16):
            t = i * 16 + p
            step = step_ref[t]
            total = total + step
            state = advance_state(state, step, drive_ref[t], rates, in_rows, t)
        return state, total

    zero = jnp.zeros((GROUP, LANES), jnp.float32)
    state, total = lax.fori_loop(0, rows // 16, advance, ((zero,) * states, zero))
    for n in range(states):
        end_ref[n] = state[n]
    end_ref[states] = total


def back_kernel(
    tok_ref, conv_ref, step_ref, drive_ref, maps_ref, decay, skip_gain, ffn_gain, *rest,
    before, final,
):
    count = max(before, 1)
    entry, rest = rest[:count], rest[count:]
    if final:
        hidden_ref, ffn_ref, kept, in_rows, out_rows, scanned = rest
    else:
        hidden_ref, ffn_ref, state_ref, kept, in_rows, out_rows, scanned = rest
    rows, width = tok_ref.shape
    states = decay.shape[0]
    tiles = width // LANES
    maps = maps_ref[...]
    spread_columns(maps, in_rows, 0, states, rows)
    spread_columns(maps, out_rows, states, states, rows)

    @pl.when(pl.program_id(0) == 0)
    def _():
        if not before:
            kept[...] = entry[0][...]
            return

        def enter(n, _):
            entering = entry[before - 1][n]
            for back in reversed(range(before - 1)):
                entering = jnp.exp2(entry[back][states] * decay[n]) * entering + entry[back][n]
            kept[n] = entering
            return 0

        lax.fori_loop(0, states, enter, 0)

    def scan_tile(k, _):
        mine = pl.ds(pl.multiple_of(k * GROUP, GROUP), GROUP)
        rates = [decay[n, mine, :] for n in range(states)]

        def advance(i, state):
            for p in range(8):
                t = i * 8 + p
                state = advance_state(state, step_ref[k, t], drive_ref[k, t], rates, in_rows, t)
                parts = [state[n] * out_rows[n, pl.ds(t, 1), :] for n in range(states)]
                while len(parts) > 1:
                    parts = [a + b for a, b in zip(parts[::2], parts[1::2])]
                scanned[k, pl.ds(pl.multiple_of(t * GROUP, GROUP), GROUP), :] = parts[0]
            return state

        state = lax.fori_loop(0, rows // 8, advance, tuple(kept[n, mine, :] for n in range(states)))
        for n in range(states):
            kept[n, mine, :] = state[n]
        return 0

    lax.fori_loop(0, tiles // GROUP, scan_tile, 0)
    if not final:
        state_ref[...] = kept[...]

    def finish(i, _):
        at = pl.multiple_of(i * 16, 16)
        squares = jnp.zeros((16, LANES), jnp.float32)
        for j in range(tiles):
            cols = pl.ds(j * LANES, LANES)
            group, lane = divmod(j, GROUP)
            came = jnp.concatenate(
                [
                    scanned[group, pl.ds((at + half * 8) * GROUP + lane, 8, stride=GROUP), :]
                    for half in range(2)
                ],
                axis=0,
            )
            conv = conv_ref[pl.ds(at, 16), cols].astype(jnp.float32)
            hidden = tok_ref[pl.ds(at, 16), cols].astype(jnp.float32) + (
                came + skip_gain[:, cols] * conv
            )
            hidden_ref[pl.ds(at, 16), cols] = hidden
            squares = squares + hidden * hidden
        mean = jnp.sum(squares, axis=-1, keepdims=True) / width
        scale = lax.rsqrt(mean + 1e-05)
        ffn_ref[pl.ds(at, 16), :] = (
            hidden_ref[pl.ds(at, 16), :] * scale * ffn_gain[...]
        ).astype(jnp.bfloat16)
        return 0

    lax.fori_loop(0, rows // 16, finish, 0)


def mixer(
    tokens, norm_gain, conv_weight, conv_bias, proj_weight, dt_weight, dt_bias, decay_rate,
    skip_gain, ffn_gain, parts, hold, note,
):
    rows, width = tokens.shape
    states = decay_rate.shape[0]
    low_width = dt_weight.shape[0]
    tiles = width // LANES
    f32, bf16 = jnp.float32, jnp.bfloat16
    shape = jax.ShapeDtypeStruct
    halo = note("h1", from_behind(tokens[rows - 16 :], "seq", 1))
    decay = (decay_rate * (-LOG2E)).reshape(states, tiles, LANES)
    row = lambda v: v.reshape(1, width)
    groups = tiles // GROUP
    wide = GROUP * LANES
    fixed = lambda v: pl.BlockSpec(v.shape, lambda k: (0,) * len(v.shape))
    slab = pl.BlockSpec((None, rows * GROUP, LANES), lambda k: (k, 0, 0))
    whole = [
        tokens, halo, row(norm_gain), conv_weight, row(conv_bias), proj_weight.T,
    ]
    conv, step, drive, maps = pl.pallas_call(
        front_kernel,
        grid=(groups,),
        out_shape=(
            shape((rows, width), bf16),
            shape((groups, rows * GROUP, LANES), f32),
            shape((groups, rows * GROUP, LANES), f32),
            shape((rows, 2 * states), f32),
        ),
        in_specs=[fixed(v) for v in whole]
        + [
            pl.BlockSpec((low_width, wide), lambda k: (0, k)),
            pl.BlockSpec((1, wide), lambda k: (0, k)),
        ],
        out_specs=(
            fixed(shape((rows, width), bf16)), slab, slab, fixed(shape((rows, 2 * states), f32)),
        ),
        scratch_shapes=[
            pltpu.VMEM((rows + 16, width), f32),
            pltpu.VMEM((rows, low_width), bf16),
            pltpu.VMEM((rows, 512), f32),
        ],
        compiler_params=params(),
        cost_estimate=cost(COST),
        name="mixer_front",
    )(*whole, dt_weight, row(dt_bias))
    conv, step, drive, maps = hold("front", conv, step, drive, maps)
    step = step.reshape(groups, rows, GROUP, LANES)
    drive = drive.reshape(groups, rows, GROUP, LANES)
    slab = pl.BlockSpec((None, rows, GROUP, LANES), lambda k: (k, 0, 0, 0))
    per_state = pl.BlockSpec((states, GROUP, LANES), lambda k: (0, k, 0))
    end = pl.pallas_call(
        ends_kernel,
        grid=(groups,),
        out_shape=shape((states + 1, tiles, LANES), f32),
        in_specs=[slab, slab, fixed(maps), per_state],
        out_specs=pl.BlockSpec((states + 1, GROUP, LANES), lambda k: (0, k, 0)),
        scratch_shapes=[pltpu.VMEM((states, rows, LANES), f32)],
        compiler_params=params(),
        cost_estimate=cost(COST),
        name="mixer_ends",
    )(step, drive, maps, decay)
    end, = hold("ends", end)
    before = lax.axis_size("seq") - 1
    ends = [note(f"e{by + 1}", from_behind(end, "seq", by + 1)) for by in range(before)]

    count = rows // parts
    piece = min(64, count)
    steps = count // piece
    outs = []
    state = None
    for part in range(parts):
        first = part * steps
        wide = pl.BlockSpec((piece, width), lambda i, first=first: (first + i, 0))
        deep = pl.BlockSpec((groups, piece, GROUP, LANES), lambda i, first=first: (0, first + i, 0, 0))
        narrow = pl.BlockSpec((piece, 2 * states), lambda i, first=first: (first + i, 0))
        whole = lambda v: pl.BlockSpec(v.shape, lambda i, r=v.ndim: (0,) * r)
        out = pl.BlockSpec((piece, width), lambda i: (i, 0))
        entry = ends if part == 0 else [state]
        final = part == parts - 1
        fixed = [decay, row(skip_gain), row(ffn_gain), *entry]
        got = pl.pallas_call(
            functools.partial(back_kernel, before=before if part == 0 else 0, final=final),
            grid=(steps,),
            out_shape=(shape((count, width), f32), shape((count, width), bf16))
            + (() if final else (shape(decay.shape, f32),)),
            in_specs=[wide, wide, deep, deep, narrow] + [whole(v) for v in fixed],
            out_specs=(out, out) + (() if final else (whole(decay),)),
            scratch_shapes=[
                pltpu.VMEM((states, tiles, LANES), f32),
                pltpu.VMEM((states, piece, LANES), f32),
                pltpu.VMEM((states, piece, LANES), f32),
                pltpu.VMEM((groups, piece * GROUP, LANES), f32),
            ],
            compiler_params=params(),
            cost_estimate=cost(COST),
            name="mixer_back",
        )(tokens, conv, step, drive, maps, *fixed)
        got = hold(f"back{part}", *got)
        outs.append(got[:2])
        state = got[2] if not final else None
    return [o[0] for o in outs], [o[1] for o in outs]


def swap(array, axis, mask):
    peers = lax.axis_size(axis)
    return lax.ppermute(array, axis, [(i, i ^ mask) for i in range(peers)])


def after(array, *others):
    return lax.optimization_barrier((array, *others))[0]


class Transfers:
    def __init__(self, w_gate, w_up, w_down):
        share = w_gate.shape[1] // lax.axis_size("seq")
        at = lax.axis_index("seq") * share
        both = jnp.concatenate(
            [lax.dynamic_slice_in_dim(w, at, share, axis=1) for w in (w_gate, w_up)], axis=1
        )
        down = lax.dynamic_slice_in_dim(w_down, at, share, axis=0)
        self.chunks = []
        for whole, sizes, axis in ((both, DEEP, 0), (down, BROAD, 1)):
            at = 0
            for size in sizes:
                self.chunks.append(lax.slice_in_dim(whole, at, at + size, axis=axis))
                at += size
        self.made = {}

    def put(self, name, array, axis, mask):
        self.made[name] = swap(self.ready(name, array), axis, mask)
        return self.made[name]

    def ready(self, name, array):
        return after(array, *[self.get(other) for other in STARTS.get(name, ())])

    def note(self, name, array):
        self.made[name] = array
        return array

    def weigh(self, chosen, route_scale):
        experts = jnp.arange(lax.axis_size("expert"), dtype=jnp.int32)[:, None, None]
        self.dense = jnp.sum(jnp.where(chosen[None] == experts, route_scale[None], 0.0), axis=2)

    def scales(self):
        if not hasattr(self, "parts"):
            me = lax.axis_index("expert")
            group = jnp.concatenate([self.dense] + [self.get(f"w{c}") for c in (2, 1, 3)], axis=1)
            both = jnp.stack([group[me], group[me ^ 4]], axis=1).reshape(4, 2, -1, 2)
            self.parts = [both[:, h].reshape(-1, 2) for h in range(2)]
        return self.parts

    def get(self, name):
        if name not in self.made:
            kind, c = name[0], int(name[1:])
            if kind == "q":
                return self.scales()[c] if c < 2 else self.chunks[len(DEEP) + c - 2]
            if kind == "w":
                send, axis, mask = self.dense, "expert", c
            elif kind == "z":
                send, axis, mask = self.chunks[c], "expert", 4
            elif kind == "x":
                send, axis, mask = self.get(f"z{c}"), "seq", 1
            elif kind == "y":
                send, axis, mask = self.get(f"z{c}"), "seq", 2
            elif c in DIRECT:
                send, axis, mask = self.get(f"z{c}"), "seq", 3
            elif c in CORNERS_X:
                send, axis, mask = self.get(f"y{c}"), "seq", 1
            else:
                send, axis, mask = self.get(f"x{c}"), "seq", 2
            self.put(name, send, axis, mask)
        return self.made[name]

    def pieces(self, c):
        return [self.get(f"{kind}{c}") for kind in "zxyc"]

    def hold(self, kernel, *arrays):
        self.made[kernel] = arrays[-1]
        others = [self.get(name) for name in WAITS.get(kernel, ())]
        return lax.optimization_barrier((*arrays, *others))[: len(arrays)]


def act_kernel(*refs, blocks, near, deep):
    xs, refs = refs[:blocks], refs[blocks:]
    fixed, refs = refs[: 2 * near], refs[2 * near :]
    pieces, refs = refs[: 4 * deep], refs[4 * deep :]
    scale, refs = refs[0], refs[1:]
    outs, refs = refs[: near + bool(deep)], refs[near + bool(deep) :]
    rows_in, held, sems = refs[0], refs[1:-1], refs[-1]
    count = xs[0].shape[0]
    copies = [(xs[b], rows_in.at[pl.ds(b * count, count), :]) for b in range(blocks)]
    copies += list(zip(fixed, held))
    first = len(copies)
    at = 0
    for c in range(deep):
        depth, both = pieces[4 * c].shape
        for origin in range(4):
            target = held[-1].at[pl.ds(at, depth), pl.ds(origin * both, both)]
            copies.append((pieces[4 * c + origin], target))
        at += depth
    copies = [pltpu.make_async_copy(a, b, sems.at[i]) for i, (a, b) in enumerate(copies)]
    for copy in copies:
        copy.start()
    for copy in copies[:first]:
        copy.wait()
    if near:
        hidden = held[0].shape[1]
        tile = hidden // 2
        for j in range(2):
            cols = slice(j * tile, (j + 1) * tile)
            g = jnp.dot(rows_in[...], held[0][:, cols], preferred_element_type=jnp.float32)
            u = jnp.dot(rows_in[...], held[1][:, cols], preferred_element_type=jnp.float32)
            outs[0][:, cols] = (silu(g) * u * scale[:, 0:1]).astype(jnp.bfloat16)
    for copy in copies[first:]:
        copy.wait()
    if deep:
        share = both // 2
        for origin in range(4):
            cols = slice(origin * both, (origin + 1) * both)
            got = jnp.dot(rows_in[...], held[-1][:, cols], preferred_element_type=jnp.float32)
            outs[-1][:, origin * share : (origin + 1) * share] = (
                silu(got[:, :share]) * got[:, share:] * scale[:, 1:2]
            ).astype(jnp.bfloat16)


def act(xs, scale, near=(), chunks=()):
    rows = sum(x.shape[0] for x in xs)
    width = xs[0].shape[1]
    pieces = [piece for chunk in chunks for piece in chunk]
    away = pl.BlockSpec(memory_space=pl.ANY)
    copies = len(xs) + len(near) + len(pieces)
    hidden = [w.shape[1] for w in near[:1]] + [2 * p.shape[1] for p in pieces[:1]]
    held = [w.shape for w in near] + [(width, 4 * p.shape[1]) for p in pieces[:1]]
    return pl.pallas_call(
        functools.partial(
            act_kernel, blocks=len(xs), near=int(bool(near)), deep=len(chunks)
        ),
        out_shape=[jax.ShapeDtypeStruct((rows, h), jnp.bfloat16) for h in hidden],
        in_specs=[away] * copies + [pl.BlockSpec(memory_space=pltpu.VMEM)],
        scratch_shapes=[pltpu.VMEM((rows, width), jnp.bfloat16)]
        + [pltpu.VMEM(shape, jnp.bfloat16) for shape in held]
        + [pltpu.SemaphoreType.DMA((copies,))],
        compiler_params=params(),
        cost_estimate=cost(COST),
        name="act",
    )(*xs, *near, *pieces, scale)


def down_kernel(*refs, halves):
    nears, fars, refs = refs[:halves], refs[halves : 2 * halves], refs[2 * halves :]
    near_weight, pieces, (keep_ref, send_ref, weight) = refs[0], refs[1:5], refs[5:]
    share = pieces[0].shape[0]
    for origin in range(4):
        weight[origin * share : (origin + 1) * share, :] = pieces[origin][...]
    rows = keep_ref.shape[0] // 2
    count = rows // halves
    for h in range(halves):
        total = jnp.dot(nears[h][...], near_weight[...], preferred_element_type=jnp.float32)
        total = total + jnp.dot(fars[h][...], weight[...], preferred_element_type=jnp.float32)
        own, ahead, mate, ahead_mate = [total[b * count : (b + 1) * count] for b in range(4)]
        keep_ref[h * count : (h + 1) * count, :] = own
        keep_ref[rows + h * count : rows + (h + 1) * count, :] = ahead
        send_ref[h * count : (h + 1) * count, :] = mate.astype(jnp.bfloat16)
        send_ref[rows + h * count : rows + (h + 1) * count, :] = ahead_mate.astype(jnp.bfloat16)


def down(nears, fars, w_down, pieces, at, skip):
    share = pieces[0].shape[0]
    hidden = w_down.shape[0]
    rows = 2 * sum(a.shape[0] // 4 for a in nears)
    tile = 512
    whole = lambda v: pl.BlockSpec(v.shape, lambda i: (0, 0))
    out = pl.BlockSpec((rows, tile), lambda i: (0, i))
    acts = [*nears, *fars]
    return pl.pallas_call(
        functools.partial(down_kernel, halves=len(nears)),
        grid=(PANEL // tile,),
        out_shape=(
            jax.ShapeDtypeStruct((rows, PANEL), jnp.float32),
            jax.ShapeDtypeStruct((rows, PANEL), jnp.bfloat16),
        ),
        in_specs=[whole(v) for v in acts]
        + [pl.BlockSpec((hidden, tile), lambda i: (0, at // tile + i))]
        + [pl.BlockSpec((share, tile), lambda i: (0, skip // tile + i)) for _ in pieces],
        out_specs=(out, out),
        scratch_shapes=[pltpu.VMEM((4 * share, tile), jnp.bfloat16)],
        compiler_params=params(),
        cost_estimate=cost(COST),
        name="down",
    )(*acts, w_down, *pieces)


def routed_by_weights(hidden, ffn_in, w_gate, w_up, w_down, moves):
    rows = hidden[0].shape[0] * len(hidden)
    halves = len(ffn_in)
    ahead = [moves.put(f"t{h}", ffn_in[h], "expert", 2) for h in range(halves)]
    parts = moves.scales()
    own = (w_gate, w_up)

    def group_rows(h):
        if MERGE:
            own = jnp.concatenate([ffn_in[h], ahead[h]], axis=0)
            return [own, moves.put(f"n{h}", own, "expert", 1)]
        mate = moves.put(f"m{h}", ffn_in[h], "expert", 1)
        return [ffn_in[h], ahead[h], mate, moves.put(f"n{h}", ahead[h], "expert", 1)]

    xs = group_rows(0)
    if TOGETHER:
        chunks = [moves.pieces(c) for c in range(len(DEEP))]
        near0, far0 = moves.hold("near0", *act(xs, parts[0], near=own, chunks=chunks))
        far0, = moves.hold("far0", far0)
    else:
        near0, = moves.hold("near0", *act(xs, parts[0], near=own))
        chunks = [moves.pieces(c) for c in range(len(DEEP))]
        far0, = moves.hold("far0", *act(xs, after(parts[0], near0), chunks=chunks))
    xs = group_rows(1)
    near1, far1 = moves.hold("act1", *act(xs, after(parts[1], far0), near=own, chunks=chunks))
    columns = []
    whole_hidden = jnp.concatenate(hidden, axis=0)
    order = [far1]
    for c, wide in enumerate(BROAD):
        pieces = moves.pieces(len(DEEP) + c)
        for skip in range(0, wide, PANEL):
            d = len(columns)
            at = d * PANEL
            held = [after(pieces[0], *order), *pieces[1:]]
            keep, send = down([near0, near1], [far0, far1], w_down, held, at, skip)
            keep, send = moves.hold(f"down{d}", keep, send)
            came = moves.put(f"s{d}", send, "expert", 1)
            order = [send, came] if IN_TURN else [send]
            came = came.astype(jnp.float32)
            back = (keep[rows:] + came[rows:]).astype(jnp.bfloat16)
            back = moves.put(f"r{d}", back, "expert", 2).astype(jnp.float32)
            total = (keep[:rows] + came[:rows]) + back
            columns.append(whole_hidden[:, at : at + PANEL] + total)
    return jnp.concatenate(columns, axis=1)


def routed_by_slots(ffn_in, chosen, route_scale, w_gate, w_up, w_down):
    tok_count, model_width = ffn_in.shape
    owners = lax.axis_size("expert")
    experts = owners * w_gate.shape[0]
    capacity = 4 * tok_count // owners
    chosen = chosen.reshape(-1)
    onehot = (chosen[:, None] == jnp.arange(experts, dtype=jnp.int32)[None, :]).astype(jnp.int32)
    before = jnp.cumsum(onehot, axis=0) - onehot
    slot_pos = jnp.sum(before * onehot, axis=1)
    dest_row = chosen * capacity + slot_pos
    outgoing = (
        jnp.zeros((experts * capacity, model_width), jnp.bfloat16)
        .at[dest_row]
        .set(jnp.repeat(ffn_in, 2, axis=0))
    )
    outgoing = outgoing.reshape(experts, capacity, model_width)
    received = lax.all_to_all(outgoing, "expert", split_axis=0, concat_axis=0, tiled=True)
    recv_shape = received.shape
    rows_in = received.reshape(-1, model_width)
    gate_part = jnp.dot(rows_in, w_gate[0], preferred_element_type=jnp.float32)
    up_part = jnp.dot(rows_in, w_up[0], preferred_element_type=jnp.float32)
    inner_act = (jax.nn.silu(gate_part) * up_part).astype(jnp.bfloat16)
    result = jnp.dot(inner_act, w_down[0], preferred_element_type=jnp.float32).astype(jnp.bfloat16)
    returned = lax.all_to_all(
        result.reshape(recv_shape), "expert", split_axis=0, concat_axis=0, tiled=True
    )
    gathered = returned.reshape(experts * capacity, model_width)[dest_row].astype(jnp.float32)
    weighted = (route_scale.reshape(-1)[:, None] * gathered).reshape(tok_count, 2, model_width)
    return weighted[:, 0] + weighted[:, 1]


def per_device(
    tokens, norm_gain, conv_weight, conv_bias, proj_weight, dt_weight, dt_bias, decay_rate,
    skip_gain, ffn_gain, expert_ids, route_weights, w_gate, w_up, w_down,
):
    by_weights = lax.axis_size("expert") == 8 and lax.axis_size("seq") == 4
    hold = lambda kernel, *arrays: arrays
    note = lambda name, array: array
    if by_weights:
        moves = Transfers(w_gate[0], w_up[0], w_down[0])
        moves.weigh(expert_ids[0], route_weights[0])
        hold, note = moves.hold, moves.note
    hidden, ffn_in = mixer(
        tokens[0], norm_gain, conv_weight, conv_bias, proj_weight, dt_weight, dt_bias,
        decay_rate, skip_gain, ffn_gain, 2 if by_weights else 1, hold, note,
    )
    if by_weights:
        out = routed_by_weights(
            hidden, ffn_in, w_gate[0], w_up[0], w_down[0], moves
        )
    else:
        out = hidden[0] + routed_by_slots(
            ffn_in[0], expert_ids[0], route_weights[0], w_gate, w_up, w_down
        )
    return out.astype(jnp.bfloat16)[None]


def solution(mesh):
    in_specs = (
        P("expert", "seq", None),
        P(), P(), P(), P(), P(), P(), P(), P(), P(),
        P("expert", "seq", None),
        P("expert", "seq", None),
        P("expert", None, None),
        P("expert", None, None),
        P("expert", None, None),
    )
    out_specs = P("expert", "seq", None)
    return jax.shard_map(
        per_device, mesh=mesh, in_specs=in_specs, out_specs=out_specs, check_vma=False
    )
```

```python
import functools
import math

import jax
import jax.numpy as jnp
from jax import lax
from jax.experimental import pallas as pl
from jax.experimental.pallas import tpu as pltpu
from jax.sharding import PartitionSpec as P

LANES = 128
GROUP = 8
LOG2E = math.log2(math.e)
VMEM_LIMIT = 56 * 2**20
COST = 0.3
MERGE = False
TOGETHER = False
IN_TURN = False
DEEP = (1024, 1024, 768, 1280)
BROAD = (2048, 1024, 1024)
PANEL = 1024
CORNERS_X = (0, 2)
DIRECT = ()
STARTS = {'z0': ['w1', 'w2', 'w3'], 'z1': ['front'], 'x0': ['front'], 'y0': ['front'], 'c0': ['ends'], 'x1': ['e1', 'e2', 'e3'], 'y1': ['e1', 'e2', 'e3'], 'z2': ['e1', 'e2', 'e3', 'z1'], 'z3': ['back0'], 'x2': ['back0'], 'y2': ['back0'], 'c1': ['back0'], 'c2': ['back1'], 'm0': ['back1'], 'z4': ['z3', 'c1'], 'x3': ['z3', 'c2'], 'y3': ['z3'], 'c3': ['near0'], 'm1': ['near0'], 'z5': ['near0', 'z4'], 'x4': ['near0'], 'y4': ['near0'], 'c4': ['far0'], 'z6': ['far0'], 'x5': ['far0'], 'y5': ['y1'], 'c5': ['act1'], 'x6': ['act1'], 'y6': ['act1'], 'c6': ['down0'], 't1': ['front'], 'r2': ['s0']}
WAITS = {'front': ['z0'], 'ends': ['x0', 'y0'], 'back0': ['c0', 'y1', 'z2'], 'back1': ['x2', 'y2', 'c1'], 'near0': ['z4', 'x3', 'y3'], 'far0': ['z5', 'y4'], 'act1': ['x4', 'z6', 'x5', 'x6'], 'down0': ['c5'], 'down1': ['c6'], 'down2': ['y5', 'y6', 'r0'], 'down3': ['c4', 'r1']}


def from_behind(array, axis, by):
    peers = lax.axis_size(axis)
    pairs = [(i, i + by) for i in range(peers) if 0 <= i + by < peers]
    return lax.ppermute(array, axis, pairs)


def silu(v):
    return v / (1.0 + jnp.exp(-v))


def softplus(v):
    return jnp.maximum(v, 0.0) + jnp.log(1.0 + jnp.exp(-jnp.abs(v)))


def spread_columns(maps, target, first, count, rows):
    for n in range(count):
        target[n] = jnp.broadcast_to(maps[:, first + n : first + n + 1], (rows, LANES))


def cost(micros):
    return pl.CostEstimate(flops=int(micros * 1.15e9), bytes_accessed=2**16, transcendentals=0)


def params():
    return pltpu.CompilerParams(vmem_limit_bytes=VMEM_LIMIT)


def front_kernel(
    tok_ref, halo_ref, norm_gain, conv_weight, conv_bias, proj_weight, dt_weight, dt_bias,
    conv_ref, step_ref, drive_ref, maps_ref,
    normed, low, block,
):
    rows, width = tok_ref.shape
    halo = halo_ref.shape[0]
    taps = conv_weight.shape[0]
    low_width = dt_weight.shape[0]
    chunk = block.shape[1]
    part = pl.program_id(0)

    @pl.when(part == 0)
    def _():
        gain = norm_gain[...]

        def norm_rows(x):
            x = x.astype(jnp.float32)
            scale = lax.rsqrt(jnp.mean(x * x, axis=-1, keepdims=True) + 1e-05)
            return (x * scale * gain).astype(jnp.bfloat16).astype(jnp.float32)

        normed[pl.ds(0, halo), :] = norm_rows(halo_ref[...])

        def norm_step(i, _):
            at = pl.multiple_of(i * 16, 16)
            normed[pl.ds(halo + at, 16), :] = norm_rows(tok_ref[pl.ds(at, 16), :])
            return 0

        lax.fori_loop(0, rows // 16, norm_step, 0)

        def conv_step(i, _):
            at = pl.multiple_of(i * 16, 16)
            for c in range(width // chunk):
                cols = pl.ds(c * chunk, chunk)
                window = normed[pl.ds(pl.multiple_of(halo - 8 + at, 8), 24), cols]
                total = jnp.zeros((16, chunk), jnp.float32)
                for j in range(taps):
                    back = taps - 1 - j
                    moved = pltpu.roll(window, back, 0) if back else window
                    total = total + conv_weight[pl.ds(j, 1), cols] * moved[8:24]
                conv_ref[pl.ds(at, 16), cols] = silu(total + conv_bias[:, cols]).astype(
                    jnp.bfloat16
                )
            return 0

        lax.fori_loop(0, rows // 16, conv_step, 0)

        conv_all = conv_ref[...]
        project = lambda weight: lax.dot_general(
            conv_all, weight, (((1,), (1,)), ((), ())), preferred_element_type=jnp.float32
        )
        low[...] = project(proj_weight[:low_width, :]).astype(jnp.bfloat16)
        maps_ref[...] = project(proj_weight[low_width:, :])

    own = dt_weight.shape[1]
    for c in range(own // chunk):
        cols = slice(c * chunk, (c + 1) * chunk)
        block[...] = softplus(
            jnp.dot(low[...], dt_weight[:, cols], preferred_element_type=jnp.float32)
            + dt_bias[:, cols]
        )
        first = pl.multiple_of(part * own + c * chunk, chunk)

        def move(g, _):
            at = pl.multiple_of(g * 16, 16)
            step = block[pl.ds(at, 16), :]
            drive = step * conv_ref[pl.ds(at, 16), pl.ds(first, chunk)].astype(jnp.float32)
            for half in range(2):
                for j in range(chunk // LANES):
                    lane = c * (chunk // LANES) + j
                    to = pl.ds((at + half * 8) * GROUP + lane, 8, stride=GROUP)
                    part = (slice(half * 8, half * 8 + 8), slice(j * LANES, (j + 1) * LANES))
                    step_ref[to, :] = step[part]
                    drive_ref[to, :] = drive[part]
            return 0

        lax.fori_loop(0, rows // 16, move, 0)


def advance_state(state, step, drive, rates, in_rows, t):
    return tuple(
        jnp.exp2(step * rates[n]) * state[n] + drive * in_rows[n, pl.ds(t, 1), :]
        for n in range(len(rates))
    )


def ends_kernel(step_ref, drive_ref, maps_ref, decay, end_ref, in_rows):
    rows = step_ref.shape[0]
    states = decay.shape[0]

    @pl.when(pl.program_id(0) == 0)
    def _():
        spread_columns(maps_ref[...], in_rows, 0, states, rows)

    rates = [decay[n] for n in range(states)]

    def advance(i, carry):
        state, total = carry
        for p in range(16):
            t = i * 16 + p
            step = step_ref[t]
            total = total + step
            state = advance_state(state, step, drive_ref[t], rates, in_rows, t)
        return state, total

    zero = jnp.zeros((GROUP, LANES), jnp.float32)
    state, total = lax.fori_loop(0, rows // 16, advance, ((zero,) * states, zero))
    for n in range(states):
        end_ref[n] = state[n]
    end_ref[states] = total


def back_kernel(
    tok_ref, conv_ref, step_ref, drive_ref, maps_ref, decay, skip_gain, ffn_gain, *rest,
    before, final,
):
    count = max(before, 1)
    entry, rest = rest[:count], rest[count:]
    if final:
        hidden_ref, ffn_ref, kept, in_rows, out_rows, scanned = rest
    else:
        hidden_ref, ffn_ref, state_ref, kept, in_rows, out_rows, scanned = rest
    rows, width = tok_ref.shape
    states = decay.shape[0]
    tiles = width // LANES
    maps = maps_ref[...]
    spread_columns(maps, in_rows, 0, states, rows)
    spread_columns(maps, out_rows, states, states, rows)

    @pl.when(pl.program_id(0) == 0)
    def _():
        if not before:
            kept[...] = entry[0][...]
            return

        def enter(n, _):
            entering = entry[before - 1][n]
            for back in reversed(range(before - 1)):
                entering = jnp.exp2(entry[back][states] * decay[n]) * entering + entry[back][n]
            kept[n] = entering
            return 0

        lax.fori_loop(0, states, enter, 0)

    def scan_tile(k, _):
        mine = pl.ds(pl.multiple_of(k * GROUP, GROUP), GROUP)
        rates = [decay[n, mine, :] for n in range(states)]

        def advance(i, state):
            for p in range(8):
                t = i * 8 + p
                state = advance_state(state, step_ref[k, t], drive_ref[k, t], rates, in_rows, t)
                parts = [state[n] * out_rows[n, pl.ds(t, 1), :] for n in range(states)]
                while len(parts) > 1:
                    parts = [a + b for a, b in zip(parts[::2], parts[1::2])]
                scanned[k, pl.ds(pl.multiple_of(t * GROUP, GROUP), GROUP), :] = parts[0]
            return state

        state = lax.fori_loop(0, rows // 8, advance, tuple(kept[n, mine, :] for n in range(states)))
        for n in range(states):
            kept[n, mine, :] = state[n]
        return 0

    lax.fori_loop(0, tiles // GROUP, scan_tile, 0)
    if not final:
        state_ref[...] = kept[...]

    def finish(i, _):
        at = pl.multiple_of(i * 16, 16)
        squares = jnp.zeros((16, LANES), jnp.float32)
        for j in range(tiles):
            cols = pl.ds(j * LANES, LANES)
            group, lane = divmod(j, GROUP)
            came = jnp.concatenate(
                [
                    scanned[group, pl.ds((at + half * 8) * GROUP + lane, 8, stride=GROUP), :]
                    for half in range(2)
                ],
                axis=0,
            )
            conv = conv_ref[pl.ds(at, 16), cols].astype(jnp.float32)
            hidden = tok_ref[pl.ds(at, 16), cols].astype(jnp.float32) + (
                came + skip_gain[:, cols] * conv
            )
            hidden_ref[pl.ds(at, 16), cols] = hidden
            squares = squares + hidden * hidden
        mean = jnp.sum(squares, axis=-1, keepdims=True) / width
        scale = lax.rsqrt(mean + 1e-05)
        ffn_ref[pl.ds(at, 16), :] = (
            hidden_ref[pl.ds(at, 16), :] * scale * ffn_gain[...]
        ).astype(jnp.bfloat16)
        return 0

    lax.fori_loop(0, rows // 16, finish, 0)


def mixer(
    tokens, norm_gain, conv_weight, conv_bias, proj_weight, dt_weight, dt_bias, decay_rate,
    skip_gain, ffn_gain, parts, hold, note,
):
    rows, width = tokens.shape
    states = decay_rate.shape[0]
    low_width = dt_weight.shape[0]
    tiles = width // LANES
    f32, bf16 = jnp.float32, jnp.bfloat16
    shape = jax.ShapeDtypeStruct
    halo = note("h1", from_behind(tokens[rows - 16 :], "seq", 1))
    decay = (decay_rate * (-LOG2E)).reshape(states, tiles, LANES)
    row = lambda v: v.reshape(1, width)
    groups = tiles // GROUP
    wide = GROUP * LANES
    fixed = lambda v: pl.BlockSpec(v.shape, lambda k: (0,) * len(v.shape))
    slab = pl.BlockSpec((None, rows * GROUP, LANES), lambda k: (k, 0, 0))
    whole = [
        tokens, halo, row(norm_gain), conv_weight, row(conv_bias), proj_weight.T,
    ]
    conv, step, drive, maps = pl.pallas_call(
        front_kernel,
        grid=(groups,),
        out_shape=(
            shape((rows, width), bf16),
            shape((groups, rows * GROUP, LANES), f32),
            shape((groups, rows * GROUP, LANES), f32),
            shape((rows, 2 * states), f32),
        ),
        in_specs=[fixed(v) for v in whole]
        + [
            pl.BlockSpec((low_width, wide), lambda k: (0, k)),
            pl.BlockSpec((1, wide), lambda k: (0, k)),
        ],
        out_specs=(
            fixed(shape((rows, width), bf16)), slab, slab, fixed(shape((rows, 2 * states), f32)),
        ),
        scratch_shapes=[
            pltpu.VMEM((rows + 16, width), f32),
            pltpu.VMEM((rows, low_width), bf16),
            pltpu.VMEM((rows, 512), f32),
        ],
        compiler_params=params(),
        cost_estimate=cost(COST),
        name="mixer_front",
    )(*whole, dt_weight, row(dt_bias))
    conv, step, drive, maps = hold("front", conv, step, drive, maps)
    step = step.reshape(groups, rows, GROUP, LANES)
    drive = drive.reshape(groups, rows, GROUP, LANES)
    slab = pl.BlockSpec((None, rows, GROUP, LANES), lambda k: (k, 0, 0, 0))
    per_state = pl.BlockSpec((states, GROUP, LANES), lambda k: (0, k, 0))
    end = pl.pallas_call(
        ends_kernel,
        grid=(groups,),
        out_shape=shape((states + 1, tiles, LANES), f32),
        in_specs=[slab, slab, fixed(maps), per_state],
        out_specs=pl.BlockSpec((states + 1, GROUP, LANES), lambda k: (0, k, 0)),
        scratch_shapes=[pltpu.VMEM((states, rows, LANES), f32)],
        compiler_params=params(),
        cost_estimate=cost(COST),
        name="mixer_ends",
    )(step, drive, maps, decay)
    end, = hold("ends", end)
    before = lax.axis_size("seq") - 1
    ends = [note(f"e{by + 1}", from_behind(end, "seq", by + 1)) for by in range(before)]

    count = rows // parts
    piece = min(64, count)
    steps = count // piece
    outs = []
    state = None
    for part in range(parts):
        first = part * steps
        wide = pl.BlockSpec((piece, width), lambda i, first=first: (first + i, 0))
        deep = pl.BlockSpec((groups, piece, GROUP, LANES), lambda i, first=first: (0, first + i, 0, 0))
        narrow = pl.BlockSpec((piece, 2 * states), lambda i, first=first: (first + i, 0))
        whole = lambda v: pl.BlockSpec(v.shape, lambda i, r=v.ndim: (0,) * r)
        out = pl.BlockSpec((piece, width), lambda i: (i, 0))
        entry = ends if part == 0 else [state]
        final = part == parts - 1
        fixed = [decay, row(skip_gain), row(ffn_gain), *entry]
        got = pl.pallas_call(
            functools.partial(back_kernel, before=before if part == 0 else 0, final=final),
            grid=(steps,),
            out_shape=(shape((count, width), f32), shape((count, width), bf16))
            + (() if final else (shape(decay.shape, f32),)),
            in_specs=[wide, wide, deep, deep, narrow] + [whole(v) for v in fixed],
            out_specs=(out, out) + (() if final else (whole(decay),)),
            scratch_shapes=[
                pltpu.VMEM((states, tiles, LANES), f32),
                pltpu.VMEM((states, piece, LANES), f32),
                pltpu.VMEM((states, piece, LANES), f32),
                pltpu.VMEM((groups, piece * GROUP, LANES), f32),
            ],
            compiler_params=params(),
            cost_estimate=cost(COST),
            name="mixer_back",
        )(tokens, conv, step, drive, maps, *fixed)
        got = hold(f"back{part}", *got)
        outs.append(got[:2])
        state = got[2] if not final else None
    return [o[0] for o in outs], [o[1] for o in outs]


def swap(array, axis, mask):
    peers = lax.axis_size(axis)
    return lax.ppermute(array, axis, [(i, i ^ mask) for i in range(peers)])


def after(array, *others):
    return lax.optimization_barrier((array, *others))[0]


class Transfers:
    def __init__(self, w_gate, w_up, w_down):
        share = w_gate.shape[1] // lax.axis_size("seq")
        at = lax.axis_index("seq") * share
        both = jnp.concatenate(
            [lax.dynamic_slice_in_dim(w, at, share, axis=1) for w in (w_gate, w_up)], axis=1
        )
        down = lax.dynamic_slice_in_dim(w_down, at, share, axis=0)
        self.chunks = []
        for whole, sizes, axis in ((both, DEEP, 0), (down, BROAD, 1)):
            at = 0
            for size in sizes:
                self.chunks.append(lax.slice_in_dim(whole, at, at + size, axis=axis))
                at += size
        self.made = {}

    def put(self, name, array, axis, mask):
        self.made[name] = swap(self.ready(name, array), axis, mask)
        return self.made[name]

    def ready(self, name, array):
        return after(array, *[self.get(other) for other in STARTS.get(name, ())])

    def note(self, name, array):
        self.made[name] = array
        return array

    def weigh(self, chosen, route_scale):
        experts = jnp.arange(lax.axis_size("expert"), dtype=jnp.int32)[:, None, None]
        self.dense = jnp.sum(jnp.where(chosen[None] == experts, route_scale[None], 0.0), axis=2)

    def scales(self):
        if not hasattr(self, "parts"):
            me = lax.axis_index("expert")
            group = jnp.concatenate([self.dense] + [self.get(f"w{c}") for c in (2, 1, 3)], axis=1)
            both = jnp.stack([group[me], group[me ^ 4]], axis=1).reshape(4, 2, -1, 2)
            self.parts = [both[:, h].reshape(-1, 2) for h in range(2)]
        return self.parts

    def get(self, name):
        if name not in self.made:
            kind, c = name[0], int(name[1:])
            if kind == "q":
                return self.scales()[c] if c < 2 else self.chunks[len(DEEP) + c - 2]
            if kind == "w":
                send, axis, mask = self.dense, "expert", c
            elif kind == "z":
                send, axis, mask = self.chunks[c], "expert", 4
            elif kind == "x":
                send, axis, mask = self.get(f"z{c}"), "seq", 1
            elif kind == "y":
                send, axis, mask = self.get(f"z{c}"), "seq", 2
            elif c in DIRECT:
                send, axis, mask = self.get(f"z{c}"), "seq", 3
            elif c in CORNERS_X:
                send, axis, mask = self.get(f"y{c}"), "seq", 1
            else:
                send, axis, mask = self.get(f"x{c}"), "seq", 2
            self.put(name, send, axis, mask)
        return self.made[name]

    def pieces(self, c):
        return [self.get(f"{kind}{c}") for kind in "zxyc"]

    def hold(self, kernel, *arrays):
        self.made[kernel] = arrays[-1]
        others = [self.get(name) for name in WAITS.get(kernel, ())]
        return lax.optimization_barrier((*arrays, *others))[: len(arrays)]


def act_kernel(*refs, blocks, near, deep):
    xs, refs = refs[:blocks], refs[blocks:]
    fixed, refs = refs[: 2 * near], refs[2 * near :]
    pieces, refs = refs[: 4 * deep], refs[4 * deep :]
    scale, refs = refs[0], refs[1:]
    outs, refs = refs[: near + bool(deep)], refs[near + bool(deep) :]
    rows_in, held, sems = refs[0], refs[1:-1], refs[-1]
    count = xs[0].shape[0]
    made = []

    def bring(source, target):
        made.append(pltpu.make_async_copy(source, target, sems.at[len(made)]))
        made[-1].start()
        return made[-1]

    first = [bring(xs[b], rows_in.at[pl.ds(b * count, count), :]) for b in range(blocks)]
    halves = [[], []]
    if near:
        hidden = held[0].shape[1]
        tile = hidden // 2
        for j in range(2):
            cols = pl.ds(j * tile, tile)
            halves[j] = [bring(w.at[:, cols], h.at[:, cols]) for w, h in zip(fixed, held)]
    if near:
        for copy in first + halves[0]:
            copy.wait()
    quarters = [[] for _ in range(4)]
    for origin in range(4 if deep else 0):
        at = 0
        for c in range(deep):
            depth, both = pieces[4 * c].shape
            target = held[-1].at[pl.ds(at, depth), pl.ds(origin * both, both)]
            quarters[origin].append(bring(pieces[4 * c + origin], target))
            at += depth
    if near:
        for j in range(2):
            cols = slice(j * tile, (j + 1) * tile)
            for copy in halves[j] if j else ():
                copy.wait()
            g = jnp.dot(rows_in[...], held[0][:, cols], preferred_element_type=jnp.float32)
            u = jnp.dot(rows_in[...], held[1][:, cols], preferred_element_type=jnp.float32)
            outs[0][:, cols] = (silu(g) * u * scale[:, 0:1]).astype(jnp.bfloat16)
    else:
        for copy in first:
            copy.wait()
    if deep:
        share = both // 2
        for copy in sum(quarters, []):
            copy.wait()
        for origin in range(4):
            cols = slice(origin * both, (origin + 1) * both)
            got = jnp.dot(rows_in[...], held[-1][:, cols], preferred_element_type=jnp.float32)
            outs[-1][:, origin * share : (origin + 1) * share] = (
                silu(got[:, :share]) * got[:, share:] * scale[:, 1:2]
            ).astype(jnp.bfloat16)


def act(xs, scale, near=(), chunks=()):
    rows = sum(x.shape[0] for x in xs)
    width = xs[0].shape[1]
    pieces = [piece for chunk in chunks for piece in chunk]
    away = pl.BlockSpec(memory_space=pl.ANY)
    away_count = len(xs) + len(near) + len(pieces)
    copies = away_count + len(near)
    hidden = [w.shape[1] for w in near[:1]] + [2 * p.shape[1] for p in pieces[:1]]
    held = [w.shape for w in near] + [(width, 4 * p.shape[1]) for p in pieces[:1]]
    return pl.pallas_call(
        functools.partial(
            act_kernel, blocks=len(xs), near=int(bool(near)), deep=len(chunks)
        ),
        out_shape=[jax.ShapeDtypeStruct((rows, h), jnp.bfloat16) for h in hidden],
        in_specs=[away] * away_count + [pl.BlockSpec(memory_space=pltpu.VMEM)],
        scratch_shapes=[pltpu.VMEM((rows, width), jnp.bfloat16)]
        + [pltpu.VMEM(shape, jnp.bfloat16) for shape in held]
        + [pltpu.SemaphoreType.DMA((copies,))],
        compiler_params=params(),
        cost_estimate=cost(COST),
        name="act",
    )(*xs, *near, *pieces, scale)


def down_kernel(*refs, halves):
    nears, fars, refs = refs[:halves], refs[halves : 2 * halves], refs[2 * halves :]
    near_weight, pieces, (keep_ref, send_ref, weight) = refs[0], refs[1:5], refs[5:]
    share = pieces[0].shape[0]
    for origin in range(4):
        weight[origin * share : (origin + 1) * share, :] = pieces[origin][...]
    rows = keep_ref.shape[0] // 2
    count = rows // halves
    for h in range(halves):
        total = jnp.dot(nears[h][...], near_weight[...], preferred_element_type=jnp.float32)
        total = total + jnp.dot(fars[h][...], weight[...], preferred_element_type=jnp.float32)
        own, ahead, mate, ahead_mate = [total[b * count : (b + 1) * count] for b in range(4)]
        keep_ref[h * count : (h + 1) * count, :] = own
        keep_ref[rows + h * count : rows + (h + 1) * count, :] = ahead
        send_ref[h * count : (h + 1) * count, :] = mate.astype(jnp.bfloat16)
        send_ref[rows + h * count : rows + (h + 1) * count, :] = ahead_mate.astype(jnp.bfloat16)


def down(nears, fars, w_down, pieces, at, skip):
    share = pieces[0].shape[0]
    hidden = w_down.shape[0]
    rows = 2 * sum(a.shape[0] // 4 for a in nears)
    tile = 512
    whole = lambda v: pl.BlockSpec(v.shape, lambda i: (0, 0))
    out = pl.BlockSpec((rows, tile), lambda i: (0, i))
    acts = [*nears, *fars]
    return pl.pallas_call(
        functools.partial(down_kernel, halves=len(nears)),
        grid=(PANEL // tile,),
        out_shape=(
            jax.ShapeDtypeStruct((rows, PANEL), jnp.float32),
            jax.ShapeDtypeStruct((rows, PANEL), jnp.bfloat16),
        ),
        in_specs=[whole(v) for v in acts]
        + [pl.BlockSpec((hidden, tile), lambda i: (0, at // tile + i))]
        + [pl.BlockSpec((share, tile), lambda i: (0, skip // tile + i)) for _ in pieces],
        out_specs=(out, out),
        scratch_shapes=[pltpu.VMEM((4 * share, tile), jnp.bfloat16)],
        compiler_params=params(),
        cost_estimate=cost(COST),
        name="down",
    )(*acts, w_down, *pieces)


def routed_by_weights(hidden, ffn_in, w_gate, w_up, w_down, moves):
    rows = hidden[0].shape[0] * len(hidden)
    halves = len(ffn_in)
    ahead = [moves.put(f"t{h}", ffn_in[h], "expert", 2) for h in range(halves)]
    parts = moves.scales()
    own = (w_gate, w_up)

    def group_rows(h):
        if MERGE:
            own = jnp.concatenate([ffn_in[h], ahead[h]], axis=0)
            return [own, moves.put(f"n{h}", own, "expert", 1)]
        mate = moves.put(f"m{h}", ffn_in[h], "expert", 1)
        return [ffn_in[h], ahead[h], mate, moves.put(f"n{h}", ahead[h], "expert", 1)]

    xs = group_rows(0)
    if TOGETHER:
        chunks = [moves.pieces(c) for c in range(len(DEEP))]
        near0, far0 = moves.hold("near0", *act(xs, parts[0], near=own, chunks=chunks))
        far0, = moves.hold("far0", far0)
    else:
        near0, = moves.hold("near0", *act(xs, parts[0], near=own))
        chunks = [moves.pieces(c) for c in range(len(DEEP))]
        far0, = moves.hold("far0", *act(xs, after(parts[0], near0), chunks=chunks))
    xs = group_rows(1)
    near1, far1 = moves.hold("act1", *act(xs, after(parts[1], far0), near=own, chunks=chunks))
    columns = []
    whole_hidden = jnp.concatenate(hidden, axis=0)
    order = [far1]
    for c, wide in enumerate(BROAD):
        pieces = moves.pieces(len(DEEP) + c)
        for skip in range(0, wide, PANEL):
            d = len(columns)
            at = d * PANEL
            held = [after(pieces[0], *order), *pieces[1:]]
            keep, send = down([near0, near1], [far0, far1], w_down, held, at, skip)
            keep, send = moves.hold(f"down{d}", keep, send)
            came = moves.put(f"s{d}", send, "expert", 1)
            order = [send, came] if IN_TURN else [send]
            came = came.astype(jnp.float32)
            back = (keep[rows:] + came[rows:]).astype(jnp.bfloat16)
            back = moves.put(f"r{d}", back, "expert", 2).astype(jnp.float32)
            total = (keep[:rows] + came[:rows]) + back
            columns.append(whole_hidden[:, at : at + PANEL] + total)
    return jnp.concatenate(columns, axis=1)


def routed_by_slots(ffn_in, chosen, route_scale, w_gate, w_up, w_down):
    tok_count, model_width = ffn_in.shape
    owners = lax.axis_size("expert")
    experts = owners * w_gate.shape[0]
    capacity = 4 * tok_count // owners
    chosen = chosen.reshape(-1)
    onehot = (chosen[:, None] == jnp.arange(experts, dtype=jnp.int32)[None, :]).astype(jnp.int32)
    before = jnp.cumsum(onehot, axis=0) - onehot
    slot_pos = jnp.sum(before * onehot, axis=1)
    dest_row = chosen * capacity + slot_pos
    outgoing = (
        jnp.zeros((experts * capacity, model_width), jnp.bfloat16)
        .at[dest_row]
        .set(jnp.repeat(ffn_in, 2, axis=0))
    )
    outgoing = outgoing.reshape(experts, capacity, model_width)
    received = lax.all_to_all(outgoing, "expert", split_axis=0, concat_axis=0, tiled=True)
    recv_shape = received.shape
    rows_in = received.reshape(-1, model_width)
    gate_part = jnp.dot(rows_in, w_gate[0], preferred_element_type=jnp.float32)
    up_part = jnp.dot(rows_in, w_up[0], preferred_element_type=jnp.float32)
    inner_act = (jax.nn.silu(gate_part) * up_part).astype(jnp.bfloat16)
    result = jnp.dot(inner_act, w_down[0], preferred_element_type=jnp.float32).astype(jnp.bfloat16)
    returned = lax.all_to_all(
        result.reshape(recv_shape), "expert", split_axis=0, concat_axis=0, tiled=True
    )
    gathered = returned.reshape(experts * capacity, model_width)[dest_row].astype(jnp.float32)
    weighted = (route_scale.reshape(-1)[:, None] * gathered).reshape(tok_count, 2, model_width)
    return weighted[:, 0] + weighted[:, 1]


def per_device(
    tokens, norm_gain, conv_weight, conv_bias, proj_weight, dt_weight, dt_bias, decay_rate,
    skip_gain, ffn_gain, expert_ids, route_weights, w_gate, w_up, w_down,
):
    by_weights = lax.axis_size("expert") == 8 and lax.axis_size("seq") == 4
    hold = lambda kernel, *arrays: arrays
    note = lambda name, array: array
    if by_weights:
        moves = Transfers(w_gate[0], w_up[0], w_down[0])
        moves.weigh(expert_ids[0], route_weights[0])
        hold, note = moves.hold, moves.note
    hidden, ffn_in = mixer(
        tokens[0], norm_gain, conv_weight, conv_bias, proj_weight, dt_weight, dt_bias,
        decay_rate, skip_gain, ffn_gain, 2 if by_weights else 1, hold, note,
    )
    if by_weights:
        out = routed_by_weights(
            hidden, ffn_in, w_gate[0], w_up[0], w_down[0], moves
        )
    else:
        out = hidden[0] + routed_by_slots(
            ffn_in[0], expert_ids[0], route_weights[0], w_gate, w_up, w_down
        )
    return out.astype(jnp.bfloat16)[None]


def solution(mesh):
    in_specs = (
        P("expert", "seq", None),
        P(), P(), P(), P(), P(), P(), P(), P(), P(),
        P("expert", "seq", None),
        P("expert", "seq", None),
        P("expert", None, None),
        P("expert", None, None),
        P("expert", None, None),
    )
    out_specs = P("expert", "seq", None)
    return jax.shard_map(
        per_device, mesh=mesh, in_specs=in_specs, out_specs=out_specs, check_vma=False
    )
```
